32 devices in a mesh: parts: 2 (over x), dp: 2 (over core), tensor: 8 (over z, y).
Axes of the slice: x: 2, y: 2, z: 4, core: 2. Of those that a mesh axis runs over, the one named last changes fastest.
Arguments:
- queries: bfloat16 [256, 64, 128], P(('parts', 'dp'), 'tensor'), parts along dimension 0, may hold values from -600 to 600
- cached_key_rows: bfloat16 [256, 8, 768, 128], P(('parts', 'dp'), None, 'tensor'), parts along dimension 0, may hold values from -6 to 6
- cached_value_rows: bfloat16 [256, 8, 768, 128], P(('parts', 'dp'), None, 'tensor'), parts along dimension 0, may hold values from -6 to 6
- cache_live_length: int32 [256], P(('parts', 'dp')), parts along dimension 0, may hold values from 2 to 768
- adapter_index: int32 [256], P(('parts', 'dp')), parts along dimension 0, may hold values from 0 to 15
- adapter_slot_index: int32 [16], replicated, may hold values from 0 to 15, each once
- output_weight: bfloat16 [8192, 8192], P('tensor'), may hold values from -0.0625 to 0.0625
- adapter_down_weight: bfloat16 [16, 8192, 64], P('dp', 'tensor'), may hold values from -0.0625 to 0.0625
- adapter_up_weight: bfloat16 [16, 64, 8192], P('dp', None, 'tensor'), may hold values from -0.75 to 0.75
Outputs:
- mixed: bfloat16 [256, 8192], P(('parts', 'dp'), 'tensor'), parts along dimension 0
The draws below stay inside these ranges and needn't reach their ends.
There are 2 independent parts, one for each index of `parts`. The reference program is written for one: setup_inputs(seed, part) draws one part's arguments, and reference() takes and returns one part's arrays. A program takes and returns all parts, laid end to end along the dimension named above; an argument that names none is the same for every part. Nothing has to cross between parts.
All inputs are finite; a program needn't handle non-finite values.
Results may differ from the reference program's by a relative error of at most 0.0061.
Values may be sent and summed in bfloat16 or wider, within the bound.
No kernel may reach another device: no remote copies, remote signals or barrier semaphores. Data moves between devices by JAX's collectives and lax.ppermute only.
A program may use at most 128 MiB of HBM per device.

```python
import math
import jax
import jax.numpy as jnp
import numpy as np
from jax import lax

MODEL_WIDTH = 8192
QUERY_HEADS = 64
HEAD_WIDTH = 128
KV_SLOTS = 8
ADAPTER_RANK = 64
L_MAX = 768
ADAPTER_COUNT = 16
REQS = 128


def anchor_rows(key):
    first = jax.random.fold_in(key, 0)
    head_key = jnp.clip(jax.random.normal(first, (REQS, KV_SLOTS, HEAD_WIDTH), jnp.float32), -4.0, 4.0)
    return head_key


def draw_cached_key_rows(key, part):
    head_key = anchor_rows(key)
    key = jax.random.fold_in(key, 3)
    keys = jnp.clip(jax.random.normal(key, (REQS, KV_SLOTS, L_MAX, HEAD_WIDTH), jnp.float32), -6.0, 6.0)
    keys = keys.at[:, :, 0, :].set(head_key)
    return keys.astype(jnp.bfloat16)


def draw_queries(key, part):
    key = jax.random.fold_in(key, 5)
    queries = jnp.clip(jax.random.normal(key, (REQS, QUERY_HEADS, HEAD_WIDTH), jnp.float32), -6.0, 6.0)
    return queries.astype(jnp.bfloat16)


def draw_cache_live_length(key, part):
    key = jax.random.fold_in(key, 9)
    lengths = jax.random.randint(key, (REQS,), 2, L_MAX + 1, jnp.int32)
    return lengths.at[0].set(L_MAX)


def with_ends(drawn, own_key, least, largest):
    spot = [jax.random.randint(jax.random.fold_in(own_key, axis), (), 0, length) for axis, length in enumerate(drawn.shape)]
    widest = drawn.shape.index(max(drawn.shape))
    neighbour = spot[:widest] + [(spot[widest] + 1) % drawn.shape[widest]] + spot[widest + 1:]
    return drawn.at[tuple(spot)].set(least).at[tuple(neighbour)].set(largest)


def shard_levels(own_key, dims, shards, low, high):
    loudness, own = 1.0, jax.random.fold_in(own_key, 6)
    for dim, blocks in shards:
        draws = jnp.exp(jax.random.uniform(jax.random.fold_in(own, dim), (blocks,), jnp.float32, low / len(shards), high / len(shards)))
        loudness = loudness * jnp.repeat(draws, dims[dim] // blocks).reshape([-1 if axis == dim else 1 for axis in range(len(dims))])
    return loudness


def rank_table(amount, slope):
    loads = [(1 << 20) // math.isqrt(grade ** slope) + 1 for grade in range(1, amount + 1)]
    deviation = 1 + sum(loads) // (1 << 30)
    return np.cumsum(np.array([max(1, weight // deviation) for weight in loads]))


def ranked(key, dims, count, lean):
    listing = rank_table(count, lean)
    pick = jax.random.randint(jax.random.fold_in(key, 1), dims, 0, int(listing[count - 1]))
    grade = jnp.searchsorted(jnp.asarray(listing, jnp.int32), pick, side="right")
    return jax.random.permutation(jax.random.fold_in(key, 2), count)[grade].astype(jnp.int32)


def gaussian(stream_key, dims, width, bound, shards=(), kind=jnp.bfloat16):
    values = width * jax.random.normal(stream_key, dims, jnp.float32)
    if shards:
        values = values * shard_levels(stream_key, dims, shards, -0.22, 0.18)
    return jnp.clip(values, -bound, bound).astype(kind)


def setup_inputs(seed: int = 0, part: int = 0) -> dict:
    key_list = jax.random.split(jax.random.key(seed), 10)
    own_keys = jax.random.split(jax.random.fold_in(key_list[9], part), 10)
    queries = draw_queries(jax.random.fold_in(jax.random.fold_in(key_list[9], part), 71), part)
    cached_key_rows = draw_cached_key_rows(jax.random.fold_in(jax.random.fold_in(key_list[9], part), 71), part)
    cached_value_rows = gaussian(own_keys[2], (REQS, KV_SLOTS, L_MAX, HEAD_WIDTH), 1.0, 6.0, ((0, 2), (2, 8)))
    cache_live_length = draw_cache_live_length(jax.random.fold_in(jax.random.fold_in(key_list[9], part), 71), part)
    adapter_index = with_ends(ranked(own_keys[4], (REQS,), ADAPTER_COUNT, 2), jax.random.fold_in(own_keys[4], 3), 0, ADAPTER_COUNT - 1).astype(jnp.int32)
    adapter_slot_index = jax.random.permutation(key_list[5], ADAPTER_COUNT).astype(jnp.int32)
    output_weight = gaussian(key_list[6], (QUERY_HEADS * HEAD_WIDTH, MODEL_WIDTH), (QUERY_HEADS * HEAD_WIDTH) ** -0.5, 0.0625, ((0, 8),))
    adapter_down_weight = gaussian(key_list[7], (ADAPTER_COUNT, QUERY_HEADS * HEAD_WIDTH, ADAPTER_RANK), (QUERY_HEADS * HEAD_WIDTH) ** -0.5, 0.0625, ((0, 2), (1, 8)))
    adapter_up_weight = gaussian(key_list[8], (ADAPTER_COUNT, ADAPTER_RANK, MODEL_WIDTH), ADAPTER_RANK ** -0.5, 0.75, ((0, 2), (2, 8)))
    return dict(queries=queries, cached_key_rows=cached_key_rows, cached_value_rows=cached_value_rows, cache_live_length=cache_live_length, adapter_index=adapter_index, adapter_slot_index=adapter_slot_index, output_weight=output_weight, adapter_down_weight=adapter_down_weight, adapter_up_weight=adapter_up_weight)


def attend_block(block):
    query, keys, values, lengths = block
    group = QUERY_HEADS // KV_SLOTS
    rows = query.shape[0]
    query = query.astype(jnp.float32).reshape(rows, KV_SLOTS, group, HEAD_WIDTH)
    scores = jnp.einsum('bsgd,bsld->bsgl', query, keys.astype(jnp.float32)) * (1.0 / math.sqrt(HEAD_WIDTH))
    live = jnp.arange(L_MAX, dtype=jnp.int32)[None, :] < lengths[:, None]
    scores = jnp.where(live[:, None, None, :], scores, -1e+30)
    top = lax.optimization_barrier(jnp.max(scores, axis=-1, keepdims=True))
    expo = jnp.where(live[:, None, None, :], jnp.exp(scores - top), 0.0)
    weights = (expo / lax.optimization_barrier(jnp.sum(expo, axis=-1, keepdims=True))).astype(jnp.bfloat16)
    attention_output = jnp.einsum('bsgl,bsld->bsgd', weights.astype(jnp.float32), values.astype(jnp.float32))
    return attention_output.reshape(rows, QUERY_HEADS * HEAD_WIDTH).astype(jnp.bfloat16)

def reference(queries, cached_key_rows, cached_value_rows, cache_live_length, adapter_index, adapter_slot_index, output_weight, adapter_down_weight, adapter_up_weight):
    blocks = REQS // 8
    attention_output = lax.map(attend_block, (queries.reshape(blocks, 8, QUERY_HEADS, HEAD_WIDTH), cached_key_rows.reshape(blocks, 8, KV_SLOTS, L_MAX, HEAD_WIDTH), cached_value_rows.reshape(blocks, 8, KV_SLOTS, L_MAX, HEAD_WIDTH), cache_live_length.reshape(blocks, 8)))
    attention_output = attention_output.reshape(REQS, QUERY_HEADS * HEAD_WIDTH)
    base_output = jnp.dot(attention_output, output_weight, preferred_element_type=jnp.float32)
    slot = adapter_slot_index[adapter_index].astype(jnp.int32)
    onehot = (slot[:, None] == jnp.arange(ADAPTER_COUNT, dtype=jnp.int32)[None, :]).astype(jnp.float32)
    gathered_partials = jnp.einsum('xl,dlo->xdo', attention_output.astype(jnp.float32), adapter_down_weight.astype(jnp.float32))
    shrink = lax.optimization_barrier(jnp.sum(gathered_partials * onehot[:, :, None], axis=1)).astype(jnp.bfloat16)
    expanded_heads = shrink.astype(jnp.float32)[:, None, :] * onehot[:, :, None]
    adapter_output = jnp.einsum('tbz,bzy->ty', expanded_heads, adapter_up_weight.astype(jnp.float32))
    return (base_output + adapter_output).astype(jnp.bfloat16)
```

```python
import functools
import math

import jax
import jax.numpy as jnp
from jax import lax
from jax.experimental import pallas as pl
from jax.experimental.pallas import tpu as pltpu
from jax.sharding import PartitionSpec as P

F32, BF16 = jnp.float32, jnp.bfloat16
DEAD = -1e30
LANES = 128
TILE = 16
VMEM_BYTES = 40 * 1024 * 1024


def call(body, grid, in_specs, out_shape, out_specs, scratch=(), prefetch=1, cost=None):
    return pl.pallas_call(
        body,
        grid_spec=pltpu.PrefetchScalarGridSpec(
            num_scalar_prefetch=prefetch,
            grid=grid,
            in_specs=in_specs,
            out_specs=out_specs,
            scratch_shapes=list(scratch),
        ),
        out_shape=out_shape,
        compiler_params=pltpu.CompilerParams(vmem_limit_bytes=VMEM_BYTES),
        cost_estimate=cost,
    )


def whole(shape):
    return pl.BlockSpec(shape, lambda i, *_: (0,) * len(shape))


def split2(x):
    high = x.astype(BF16).astype(F32)
    return high, (x - high).astype(BF16).astype(F32)


def iota(shape, dim):
    return lax.broadcasted_iota(jnp.int32, shape, dim)


def attend_body(steps, heads, scale, sc_ref, q_ref, k_ref, v_ref, o_ref):
    step = pl.program_id(0)
    reqs, positions = k_ref.shape[0], k_ref.shape[2]
    per_tile = TILE // heads
    tiles = reqs // per_tile
    body_rows = steps * tiles * TILE
    row = iota((TILE, LANES), 0) // heads
    lane = iota((TILE, LANES), 1)
    pos = iota((TILE, positions), 1)
    prow = iota((TILE, positions), 0) // heads
    stat = jnp.zeros((TILE, LANES), F32)
    for g in range(tiles):
        q = q_ref[pl.ds(g * TILE, TILE), :]
        zero = jnp.zeros_like(q)
        left = jnp.concatenate([jnp.where(row == a, q, zero) for a in range(per_tile)], axis=1)
        right = jnp.concatenate([k_ref[g * per_tile + a, 0] for a in range(per_tile)], axis=1)
        s = lax.dot_general(left, right, (((1,), (1,)), ((), ())), preferred_element_type=F32) * scale
        first = step * reqs + g * per_tile
        live = jnp.zeros((TILE, positions), jnp.int32)
        for a in range(per_tile):
            live = jnp.where(prow == a, sc_ref[1 + first + a], live)
        alive = pos < live
        s = jnp.where(alive, s, DEAD)
        high, mid = split2(jnp.max(s, axis=1, keepdims=True))
        p = jnp.where(alive, jnp.exp(s - (high + mid)), 0.0)
        lhigh, lmid = split2(jnp.sum(p, axis=1, keepdims=True))
        values = jnp.concatenate([v_ref[g * per_tile + a, 0] for a in range(per_tile)], axis=1)
        wide = jnp.dot(p.astype(BF16), values, preferred_element_type=F32)
        acc = wide[:, :LANES]
        for a in range(1, per_tile):
            acc = jnp.where(row == a, wide[:, a * LANES : (a + 1) * LANES], acc)
        o_ref[pl.ds(pl.multiple_of((step * tiles + g) * TILE, TILE), TILE), :] = acc.astype(BF16)
        at = 4 * (step * tiles + g)
        for n, val in enumerate((high, mid, lhigh, lmid)):
            stat = jnp.where(lane == at + n, val, stat)

    @pl.when(step == 0)
    def _():
        o_ref[pl.ds(body_rows, TILE), :] = stat.astype(BF16)

    @pl.when(step > 0)
    def _():
        o_ref[pl.ds(body_rows, TILE), :] = (o_ref[pl.ds(body_rows, TILE), :].astype(F32) + stat).astype(BF16)


def attend(scalars, q, keys, values, heads, scale):
    rows, _, positions, width = keys.shape
    steps = 4
    block = rows // steps
    kv = pl.BlockSpec((block, 1, positions, width), lambda i, sc: (i, sc[0], 0, 0))
    n = rows * heads + TILE
    return call(
        functools.partial(attend_body, steps, heads, scale),
        (steps,),
        [pl.BlockSpec((block * heads, width), lambda i, sc: (i, 0)), kv, kv],
        jax.ShapeDtypeStruct((n, width), BF16),
        whole((n, width)),
        cost=pl.CostEstimate(
            flops=4 * rows * heads * positions * width * 8,
            bytes_accessed=4 * rows * positions * width,
            transcendentals=rows * heads * positions,
        ),
    )(scalars, q, keys, values)


def combine(stats):
    tops = [s + pltpu.roll(s, LANES - 1, 1) for s in stats]
    sums = [pltpu.roll(t, LANES - 2, 1) for t in tops]
    best = functools.reduce(jnp.maximum, tops)
    weights = [jnp.exp(t - best) for t in tops]
    total = sum(w * l for w, l in zip(weights, sums))
    return best, weights, total


def pair_body(a_ref, b_ref, o_ref):
    n = a_ref.shape[0] - TILE
    sa = a_ref[pl.ds(n, TILE), :].astype(F32)
    sb = b_ref[pl.ds(n, TILE), :].astype(F32)
    lane = iota((TILE, LANES), 1) % 4
    first = lane == 0
    best, (wa, wb), total = combine([sa, sb])
    wa, wb = jnp.where(first, wa, 0.0), jnp.where(first, wb, 0.0)
    high, mid = split2(best)
    lhigh, lmid = split2(total)
    stat = jnp.where(first, high, 0.0)
    stat = jnp.where(lane == 1, pltpu.roll(mid, 1, 1), stat)
    stat = jnp.where(lane == 2, pltpu.roll(lhigh, 2, 1), stat)
    stat = jnp.where(lane == 3, pltpu.roll(lmid, 3, 1), stat)
    o_ref[pl.ds(n, TILE), :] = stat.astype(BF16)
    for g in range(n // TILE):
        at = pl.ds(g * TILE, TILE)
        o_ref[at, :] = (
            wa[:, 4 * g : 4 * g + 1] * a_ref[at, :].astype(F32)
            + wb[:, 4 * g : 4 * g + 1] * b_ref[at, :].astype(F32)
        ).astype(BF16)


def pair(a, b):
    return pl.pallas_call(
        pair_body,
        out_shape=jax.ShapeDtypeStruct(a.shape, BF16),
        compiler_params=pltpu.CompilerParams(vmem_limit_bytes=VMEM_BYTES),
        cost_estimate=pl.CostEstimate(flops=3 * a.size, bytes_accessed=6 * a.size, transcendentals=0),
    )(a, b)


def finish_attention(parts, att32, att_ref, heads):
    n = parts[0].shape[0] - TILE
    stats = [p[pl.ds(n, TILE), :].astype(F32) for p in parts]
    _, weights, total = combine(stats)
    inverse = 1.0 / total
    weights = [w * inverse for w in weights]
    for g in range(n // TILE):
        at = pl.ds(g * TILE, TILE)
        att32[at, :] = sum(
            w[:, 4 * g : 4 * g + 1] * p[at, :].astype(F32) for w, p in zip(weights, parts)
        )
    for h in range(heads):
        att_ref[:, h * LANES : (h + 1) * LANES] = att32[pl.ds(h, n // heads, stride=heads), :].astype(BF16)


def chosen(rel, wide, rank):
    total = None
    lane = iota((wide.shape[0], LANES), 1)
    for b in range(wide.shape[1] // LANES):
        part = jnp.where(rel == (lane + b * LANES) // rank, wide[:, b * LANES : (b + 1) * LANES], 0.0)
        total = part if total is None else total + part
    return total


def project_body(n_parts, n_out, heads, rank, sc_ref, *refs):
    parts = refs[:n_parts]
    w_ref, slot_ref, down_a, down_b = refs[n_parts : n_parts + 4]
    outs = refs[n_parts + 4 : n_parts + 4 + n_out]
    att_ref, shrink_ref, att32 = refs[n_parts + 4 + n_out :]
    step = pl.program_id(0)

    @pl.when(step == 0)
    def _():
        finish_attention(parts, att32, att_ref, heads)
        att = att_ref[...]
        over = (((1,), (1,)), ((), ()))
        own = lax.dot_general(att, down_a[...], over, preferred_element_type=F32)
        other = lax.dot_general(att, down_b[...], over, preferred_element_type=F32)
        slots = slot_ref[...]
        per = down_a.shape[0] // rank
        mine = sc_ref[0]
        s = chosen(slots - mine * per, own, rank) + chosen(slots - (1 - mine) * per, other, rank)
        s = s + pltpu.roll(s, rank, 1)
        high, mid = split2(s)
        shrink_ref[...] = jnp.where(iota(s.shape, 1) < rank, high, mid).astype(BF16)

    for k in range(n_out):

        @pl.when(step == k)
        def _(k=k):
            out = jnp.dot(att_ref[...], w_ref[...], preferred_element_type=F32)
            outs[k][:, : out.shape[1]] = out.astype(BF16)
            outs[k][:, out.shape[1] :] = shrink_ref[...]


def project(scalars, parts, weight, slots, down_a, down_b, heads, rank, cols):
    n_out = scalars.shape[0] - 1
    rows = slots.shape[0]
    width = weight.shape[0]
    msg = jax.ShapeDtypeStruct((rows, cols + LANES), BF16)
    outs = call(
        functools.partial(project_body, len(parts), n_out, heads, rank),
        (n_out,),
        [whole(p.shape) for p in parts]
        + [pl.BlockSpec((width, cols), lambda i, sc: (0, sc[1 + i]))]
        + [whole(slots.shape), whole(down_a.shape), whole(down_b.shape)],
        [msg] * n_out
        + [jax.ShapeDtypeStruct((rows, width), BF16), jax.ShapeDtypeStruct((rows, LANES), BF16)],
        [whole(msg.shape)] * n_out + [whole((rows, width)), whole((rows, LANES))],
        scratch=[pltpu.VMEM((rows * heads, LANES), F32)],
        cost=pl.CostEstimate(
            flops=2 * rows * width * cols * n_out, bytes_accessed=2 * width * cols * n_out, transcendentals=0
        ),
    )(scalars, *parts, weight, slots, down_a, down_b)
    return outs[:n_out], outs[n_out], outs[n_out + 1]


def project_more_body(n_out, sc_ref, att_ref, shrink_ref, w_ref, *outs):
    step = pl.program_id(0)
    for k in range(n_out):

        @pl.when(step == k)
        def _(k=k):
            out = jnp.dot(att_ref[...], w_ref[...], preferred_element_type=F32)
            outs[k][:, : out.shape[1]] = out
            outs[k][:, out.shape[1] :] = shrink_ref[...].astype(F32)


def project_more(scalars, att, shrink, weight, cols):
    n_out = scalars.shape[0] - 1
    rows, width = att.shape
    msg = jax.ShapeDtypeStruct((rows, cols + LANES), F32)
    return call(
        functools.partial(project_more_body, n_out),
        (n_out,),
        [
            whole(att.shape),
            whole(shrink.shape),
            pl.BlockSpec((width, cols), lambda i, sc: (0, sc[1 + i])),
        ],
        [msg] * n_out,
        [whole(msg.shape)] * n_out,
        cost=pl.CostEstimate(
            flops=2 * rows * width * cols * n_out, bytes_accessed=2 * width * cols * n_out, transcendentals=0
        ),
    )(scalars, att, shrink, weight)


def shrink_sum(parts, rank):
    both = sum(parts)
    return both + pltpu.roll(both, rank, 1)


def add_body(rank, a_ref, b_ref, o_ref):
    cols = a_ref.shape[1] - LANES
    o_ref[:, :cols] = (a_ref[:, :cols] + b_ref[:, :cols].astype(F32)).astype(BF16)
    s = shrink_sum([a_ref[:, cols:], b_ref[:, cols:].astype(F32)], rank)
    high, mid = split2(s)
    o_ref[:, cols:] = jnp.where(iota(s.shape, 1) < rank, high, mid).astype(BF16)


def add(a, b, rank):
    return pl.pallas_call(
        functools.partial(add_body, rank),
        out_shape=jax.ShapeDtypeStruct(a.shape, BF16),
        compiler_params=pltpu.CompilerParams(vmem_limit_bytes=VMEM_BYTES),
        cost_estimate=pl.CostEstimate(flops=a.size, bytes_accessed=8 * a.size, transcendentals=0),
    )(a, b)


def expanded(rel, shrink, rank, width):
    lane = iota((rel.shape[0], LANES), 1)
    zero = jnp.zeros(rel.shape, F32)
    return jnp.concatenate(
        [
            jnp.where(rel == (lane + b * LANES) // rank, shrink, zero).astype(BF16)
            for b in range(width // LANES)
        ],
        axis=1,
    )


def last_body(rank, n_parts, mine_ref, slot_ref, up_a, up_b, *refs):
    parts, o_ref = refs[:n_parts], refs[n_parts]
    cols = o_ref.shape[1]
    base = sum(p[:, :cols].astype(F32) for p in parts)
    shrink = shrink_sum([p[:, cols:].astype(F32) for p in parts], rank).astype(BF16).astype(F32)
    slots = slot_ref[...]
    mine = mine_ref[0]
    per = up_a.shape[0] // rank
    xa = expanded(slots - mine * per, shrink, rank, up_a.shape[0])
    xb = expanded(slots - (1 - mine) * per, shrink, rank, up_b.shape[0])
    lora = jnp.dot(xa, up_a[...], preferred_element_type=F32) + jnp.dot(
        xb, up_b[...], preferred_element_type=F32
    )
    o_ref[...] = (base + lora).astype(BF16)


def last(mine, slots, up_a, up_b, parts, rank):
    rows, cols = slots.shape[0], up_a.shape[1]
    return call(
        functools.partial(last_body, rank, len(parts)),
        (1,),
        [whole(slots.shape), whole(up_a.shape), whole(up_b.shape)] + [whole(p.shape) for p in parts],
        jax.ShapeDtypeStruct((rows, cols), BF16),
        whole((rows, cols)),
        cost=pl.CostEstimate(flops=4 * rows * up_a.size // rows, bytes_accessed=4 * up_a.size, transcendentals=0),
    )(mine, slots, up_a, up_b, *parts)


def on_device(
    tensor,
    queries,
    cached_key_rows,
    cached_value_rows,
    cache_live_length,
    adapter_index,
    adapter_slot_index,
    output_weight,
    adapter_down_weight,
    adapter_up_weight,
):
    rows, heads, width = queries.shape
    kv_heads, positions = cached_key_rows.shape[1:3]
    group = heads * tensor // kv_heads
    slots_here, _, rank = adapter_down_weight.shape
    cols = adapter_up_weight.shape[2]
    me = lax.axis_index("tensor")
    mine = lax.axis_index("dp")

    def hop(x, k):
        return lax.ppermute(x, "tensor", [(i, i ^ k) for i in range(tensor)])

    def across(x):
        return lax.ppermute(x, "dp", [(0, 1), (1, 0)])

    far = sorted(range(2, tensor, 2), key=lambda k: -min(k, 4))
    outer = far + [0]

    q = queries.reshape(rows * heads, width)
    held = {0: q}
    held[1] = hop(q, 1)
    for k in far:
        held[k] = hop(q, k)
    for k in far:
        held[k ^ 1] = hop(held[k], 1)

    down_a = jnp.swapaxes(adapter_down_weight, 1, 2).reshape(slots_here * rank, -1)
    up_a = adapter_up_weight.reshape(slots_here * rank, cols)
    down_b, up_b = across(down_a), across(up_a)

    live = jnp.clip(cache_live_length - me * positions, 0, positions)
    scale = 1.0 / math.sqrt(width)

    def attended(k):
        head = ((me ^ k) * heads) // group
        scalars = jnp.concatenate([head[None], live]).astype(jnp.int32)
        return attend(scalars, held[k], cached_key_rows, cached_value_rows, heads, scale)

    sent = {k: hop(attended(k ^ 1), 1) for k in [0] + far}
    merged = {k: pair(attended(k), sent[k]) for k in [0] + far}
    parts = [merged[0]] + [hop(merged[k], k) for k in far]

    total_slots = adapter_slot_index.shape[0]
    match = adapter_index[:, None] == jnp.arange(total_slots, dtype=jnp.int32)[None, :]
    slot = jnp.sum(jnp.where(match, adapter_slot_index[None, :], 0), axis=1)
    slots = jnp.broadcast_to(slot[:, None], (rows, LANES)).astype(jnp.int32)

    order = jnp.array([k for k in outer], jnp.int32)
    to_pair = jnp.concatenate([mine[None], me ^ order ^ 1]).astype(jnp.int32)
    to_own = jnp.concatenate([mine[None], me ^ order]).astype(jnp.int32)
    first, att, shrink = project(
        to_pair, parts, output_weight, slots, down_a, down_b, heads, rank, cols
    )
    arrived = [hop(x, 1) for x in first]
    own = project_more(to_own, att, shrink, output_weight, cols)
    summed = [add(a, b, rank) for a, b in zip(own, arrived)]
    final = [hop(x, k) if k else x for x, k in zip(summed, outer)]
    return last(mine[None].astype(jnp.int32), slots, up_a, up_b, final, rank)


def solution(mesh):
    placed = (
        P(("parts", "dp"), "tensor", None),
        P(("parts", "dp"), None, "tensor", None),
        P(("parts", "dp"), None, "tensor", None),
        P(("parts", "dp")),
        P(("parts", "dp")),
        P(),
        P("tensor", None),
        P("dp", "tensor", None),
        P("dp", None, "tensor"),
    )
    return jax.shard_map(
        functools.partial(on_device, mesh.shape["tensor"]),
        mesh=mesh,
        in_specs=placed,
        out_specs=P(("parts", "dp"), "tensor"),
        check_vma=False,
    )
```

```python
import functools
import math

import jax
import jax.numpy as jnp
from jax import lax
from jax.experimental import pallas as pl
from jax.experimental.pallas import tpu as pltpu
from jax.sharding import PartitionSpec as P

F32, BF16 = jnp.float32, jnp.bfloat16
DEAD = -1e30
LANES = 128
TILE = 16
SMALL = 8 * 1024 * 1024
LARGE = 32 * 1024 * 1024


def call(body, grid, in_specs, out_shape, out_specs, scratch=(), prefetch=1, cost=None):
    return pl.pallas_call(
        body,
        grid_spec=pltpu.PrefetchScalarGridSpec(
            num_scalar_prefetch=prefetch,
            grid=grid,
            in_specs=in_specs,
            out_specs=out_specs,
            scratch_shapes=list(scratch),
        ),
        out_shape=out_shape,
        compiler_params=pltpu.CompilerParams(vmem_limit_bytes=SMALL),
        cost_estimate=cost,
    )


def whole(shape):
    return pl.BlockSpec(shape, lambda i, *_: (0,) * len(shape))


def split2(x):
    high = x.astype(BF16).astype(F32)
    return high, (x - high).astype(BF16).astype(F32)


def iota(shape, dim):
    return lax.broadcasted_iota(jnp.int32, shape, dim)


def attend_part(heads, scale, q, live, keys, values, first_tile, o_ref):
    rows, positions = keys.shape[0], keys.shape[1]
    per_tile = TILE // heads
    tiles = rows // per_tile
    row = iota((TILE, LANES), 0) // heads
    lane = iota((TILE, LANES), 1)
    scores = []
    for g in range(tiles):
        left = q[g * TILE : (g + 1) * TILE, :]
        zero = jnp.zeros_like(left)
        left = jnp.concatenate([jnp.where(row == a, left, zero) for a in range(per_tile)], axis=1)
        right = jnp.concatenate([keys[g * per_tile + a] for a in range(per_tile)], axis=1)
        scores.append(
            lax.dot_general(left, right, (((1,), (1,)), ((), ())), preferred_element_type=F32)
        )
    s = jnp.concatenate(scores, axis=0) * scale
    alive = iota(s.shape, 1) < live[:, :positions]
    s = jnp.where(alive, s, DEAD)
    high, mid = split2(jnp.max(s, axis=1, keepdims=True))
    p = jnp.where(alive, jnp.exp(s - (high + mid)), 0.0)
    lhigh, lmid = split2(jnp.sum(p, axis=1, keepdims=True))
    p = p.astype(BF16)
    stat = jnp.zeros((TILE, LANES), F32)
    for g in range(tiles):
        at = slice(g * TILE, (g + 1) * TILE)
        right = jnp.concatenate([values[g * per_tile + a] for a in range(per_tile)], axis=1)
        wide = jnp.dot(p[at], right, preferred_element_type=F32)
        acc = wide[:, :LANES]
        for a in range(1, per_tile):
            acc = jnp.where(row == a, wide[:, a * LANES : (a + 1) * LANES], acc)
        to = first_tile + g
        o_ref[to * TILE : (to + 1) * TILE, :] = acc.astype(BF16)
        for n, val in enumerate((high, mid, lhigh, lmid)):
            stat = jnp.where(lane == 4 * to + n, val[at], stat)
    return stat


def attend_body(n, blocks, heads, scale, sc_ref, live_ref, k_hbm, v_hbm, *refs):
    q_refs, o_refs = refs[:n], refs[n : 2 * n]
    k_buf, v_buf, k_sem, v_sem = refs[2 * n :]
    size = k_hbm.shape[0] // blocks
    copies = []
    for j in range(n):
        kv = sc_ref[j]
        for b in range(blocks):
            at, i = pl.ds(b * size, size), j * blocks + b
            copies.append(
                (
                    pltpu.make_async_copy(k_hbm.at[at, kv], k_buf.at[i], k_sem.at[i]),
                    pltpu.make_async_copy(v_hbm.at[at, kv], v_buf.at[i], v_sem.at[i]),
                )
            )
    for ck, cv in copies:
        ck.start()
        cv.start()
    many = size * heads
    for j in range(n):
        stat = jnp.zeros((TILE, LANES), F32)
        for b in range(blocks):
            i = j * blocks + b
            copies[i][0].wait()
            copies[i][1].wait()
            at = slice(b * many, (b + 1) * many)
            stat = stat + attend_part(
                heads, scale, q_refs[j][at, :], live_ref[at, :], k_buf.at[i], v_buf.at[i],
                b * many // TILE, o_refs[j],
            )
        o_refs[j][many * blocks :, :] = stat.astype(BF16)


def attend(which, queries, live, keys, values, heads, scale):
    n, blocks = len(queries), 2
    rows, _, positions, width = keys.shape
    vmem = pl.BlockSpec(memory_space=pltpu.VMEM)
    hbm = pl.BlockSpec(memory_space=pltpu.HBM)
    buf = pltpu.VMEM((n * blocks, rows // blocks, positions, width), BF16)
    sem = pltpu.SemaphoreType.DMA((n * blocks,))
    return pl.pallas_call(
        functools.partial(attend_body, n, blocks, heads, scale),
        in_specs=[pl.BlockSpec(memory_space=pltpu.SMEM), vmem, hbm, hbm] + [vmem] * n,
        out_specs=[vmem] * n,
        out_shape=[jax.ShapeDtypeStruct((rows * heads + TILE, width), BF16)] * n,
        scratch_shapes=[buf, buf, sem, sem],
        compiler_params=pltpu.CompilerParams(vmem_limit_bytes=LARGE),
        cost_estimate=pl.CostEstimate(
            flops=32 * n * rows * heads * positions * width,
            bytes_accessed=4 * n * rows * positions * width,
            transcendentals=n * rows * heads * positions,
        ),
    )(which, live, keys, values, *queries)


def combine(stats):
    tops = [s + pltpu.roll(s, LANES - 1, 1) for s in stats]
    sums = [pltpu.roll(t, LANES - 2, 1) for t in tops]
    best = functools.reduce(jnp.maximum, tops)
    weights = [jnp.exp(t - best) for t in tops]
    total = sum(w * l for w, l in zip(weights, sums))
    return best, weights, total


def pair_body(a_ref, b_ref, o_ref):
    n = a_ref.shape[0] - TILE
    sa = a_ref[pl.ds(n, TILE), :].astype(F32)
    sb = b_ref[pl.ds(n, TILE), :].astype(F32)
    lane = iota((TILE, LANES), 1) % 4
    first = lane == 0
    best, (wa, wb), total = combine([sa, sb])
    wa, wb = jnp.where(first, wa, 0.0), jnp.where(first, wb, 0.0)
    high, mid = split2(best)
    lhigh, lmid = split2(total)
    stat = jnp.where(first, high, 0.0)
    stat = jnp.where(lane == 1, pltpu.roll(mid, 1, 1), stat)
    stat = jnp.where(lane == 2, pltpu.roll(lhigh, 2, 1), stat)
    stat = jnp.where(lane == 3, pltpu.roll(lmid, 3, 1), stat)
    o_ref[pl.ds(n, TILE), :] = stat.astype(BF16)
    for g in range(n // TILE):
        at = pl.ds(g * TILE, TILE)
        o_ref[at, :] = (
            wa[:, 4 * g : 4 * g + 1] * a_ref[at, :].astype(F32)
            + wb[:, 4 * g : 4 * g + 1] * b_ref[at, :].astype(F32)
        ).astype(BF16)


def pair(a, b):
    return pl.pallas_call(
        pair_body,
        out_shape=jax.ShapeDtypeStruct(a.shape, BF16),
        compiler_params=pltpu.CompilerParams(vmem_limit_bytes=SMALL),
        cost_estimate=pl.CostEstimate(flops=3 * a.size, bytes_accessed=6 * a.size, transcendentals=0),
    )(a, b)


def finish_attention(parts, att32, att_ref, heads):
    n = parts[0].shape[0] - TILE
    stats = [p[pl.ds(n, TILE), :].astype(F32) for p in parts]
    _, weights, total = combine(stats)
    inverse = 1.0 / total
    weights = [w * inverse for w in weights]
    for g in range(n // TILE):
        at = pl.ds(g * TILE, TILE)
        att32[at, :] = sum(
            w[:, 4 * g : 4 * g + 1] * p[at, :].astype(F32) for w, p in zip(weights, parts)
        )
    for h in range(heads):
        att_ref[:, h * LANES : (h + 1) * LANES] = att32[pl.ds(h, n // heads, stride=heads), :].astype(BF16)


def chosen(rel, wide, rank):
    total = None
    lane = iota((wide.shape[0], LANES), 1)
    for b in range(wide.shape[1] // LANES):
        part = jnp.where(rel == (lane + b * LANES) // rank, wide[:, b * LANES : (b + 1) * LANES], 0.0)
        total = part if total is None else total + part
    return total


def fetch(scalars, first, w_ref, buf, sem):
    cols = buf.shape[2]
    copies = []
    for k in range(buf.shape[0]):
        at = pl.ds(pl.multiple_of(scalars[first + k] * cols, cols), cols)
        copies.append(pltpu.make_async_copy(w_ref.at[:, at], buf.at[k], sem.at[k]))
        copies[-1].start()
    return copies


def project_body(n_parts, n_out, heads, rank, sc_ref, w_ref, *refs):
    parts = refs[:n_parts]
    slot_ref, down_a, down_b = refs[n_parts : n_parts + 3]
    outs = refs[n_parts + 3 : n_parts + 3 + n_out]
    att_ref, shrink_ref, att32, buf, sem = refs[n_parts + 3 + n_out :]
    copies = fetch(sc_ref, 1, w_ref, buf, sem)
    finish_attention(parts, att32, att_ref, heads)
    att = att_ref[...]
    over = (((1,), (1,)), ((), ()))
    own = lax.dot_general(att, down_a[...], over, preferred_element_type=F32)
    other = lax.dot_general(att, down_b[...], over, preferred_element_type=F32)
    slots = slot_ref[...]
    per = down_a.shape[0] // rank
    mine = sc_ref[0]
    s = chosen(slots - mine * per, own, rank) + chosen(slots - (1 - mine) * per, other, rank)
    s = s + pltpu.roll(s, rank, 1)
    high, mid = split2(s)
    shrink = jnp.where(iota(s.shape, 1) < rank, high, mid).astype(BF16)
    shrink_ref[...] = shrink
    for k, out in enumerate(outs):
        cols = buf.shape[2]
        copies[k].wait()
        out[:, :cols] = jnp.dot(att, buf[k], preferred_element_type=F32).astype(BF16)
        out[:, cols:] = shrink


def project(scalars, parts, weight, slots, down_a, down_b, heads, rank, cols):
    n_out = scalars.shape[0] - 1
    rows = slots.shape[0]
    width = weight.shape[0]
    vmem = pl.BlockSpec(memory_space=pltpu.VMEM)
    outs = pl.pallas_call(
        functools.partial(project_body, len(parts), n_out, heads, rank),
        in_specs=[pl.BlockSpec(memory_space=pltpu.SMEM), pl.BlockSpec(memory_space=pltpu.HBM)]
        + [vmem] * (len(parts) + 3),
        out_specs=[vmem] * (n_out + 2),
        out_shape=[jax.ShapeDtypeStruct((rows, cols + LANES), BF16)] * n_out
        + [jax.ShapeDtypeStruct((rows, width), BF16), jax.ShapeDtypeStruct((rows, LANES), BF16)],
        scratch_shapes=[
            pltpu.VMEM((rows * heads, LANES), F32),
            pltpu.VMEM((n_out, width, cols), BF16),
            pltpu.SemaphoreType.DMA((n_out,)),
        ],
        compiler_params=pltpu.CompilerParams(vmem_limit_bytes=LARGE),
        cost_estimate=pl.CostEstimate(
            flops=2 * rows * width * cols * n_out, bytes_accessed=2 * width * cols * n_out, transcendentals=0
        ),
    )(scalars, weight, *parts, slots, down_a, down_b)
    return outs[:n_out], outs[n_out], outs[n_out + 1]


def project_more_body(n_out, sc_ref, w_ref, att_ref, shrink_ref, *refs):
    outs = refs[:n_out]
    buf, sem = refs[n_out:]
    copies = fetch(sc_ref, 1, w_ref, buf, sem)
    cols = buf.shape[2]
    for k, out in enumerate(outs):
        copies[k].wait()
        out[:, :cols] = jnp.dot(att_ref[...], buf[k], preferred_element_type=F32)
        out[:, cols:] = shrink_ref[...].astype(F32)


def project_more(scalars, att, shrink, weight, cols):
    n_out = scalars.shape[0] - 1
    rows, width = att.shape
    vmem = pl.BlockSpec(memory_space=pltpu.VMEM)
    return pl.pallas_call(
        functools.partial(project_more_body, n_out),
        in_specs=[pl.BlockSpec(memory_space=pltpu.SMEM), pl.BlockSpec(memory_space=pltpu.HBM), vmem, vmem],
        out_specs=[vmem] * n_out,
        out_shape=[jax.ShapeDtypeStruct((rows, cols + LANES), F32)] * n_out,
        scratch_shapes=[pltpu.VMEM((n_out, width, cols), BF16), pltpu.SemaphoreType.DMA((n_out,))],
        compiler_params=pltpu.CompilerParams(vmem_limit_bytes=LARGE),
        cost_estimate=pl.CostEstimate(
            flops=2 * rows * width * cols * n_out, bytes_accessed=2 * width * cols * n_out, transcendentals=0
        ),
    )(scalars, weight, att, shrink)


def shrink_sum(parts, rank):
    both = sum(parts)
    return both + pltpu.roll(both, rank, 1)


def add_body(rank, a_ref, b_ref, o_ref):
    cols = a_ref.shape[1] - LANES
    o_ref[:, :cols] = (a_ref[:, :cols] + b_ref[:, :cols].astype(F32)).astype(BF16)
    s = shrink_sum([a_ref[:, cols:], b_ref[:, cols:].astype(F32)], rank)
    high, mid = split2(s)
    o_ref[:, cols:] = jnp.where(iota(s.shape, 1) < rank, high, mid).astype(BF16)


def add(a, b, rank):
    return pl.pallas_call(
        functools.partial(add_body, rank),
        out_shape=jax.ShapeDtypeStruct(a.shape, BF16),
        compiler_params=pltpu.CompilerParams(vmem_limit_bytes=SMALL),
        cost_estimate=pl.CostEstimate(flops=a.size, bytes_accessed=8 * a.size, transcendentals=0),
    )(a, b)


def expanded(rel, shrink, rank, width):
    lane = iota((rel.shape[0], LANES), 1)
    zero = jnp.zeros(rel.shape, F32)
    return jnp.concatenate(
        [
            jnp.where(rel == (lane + b * LANES) // rank, shrink, zero).astype(BF16)
            for b in range(width // LANES)
        ],
        axis=1,
    )


def last_body(rank, n_parts, mine_ref, slot_ref, up_a, up_b, *refs):
    parts, o_ref = refs[:n_parts], refs[n_parts]
    cols = o_ref.shape[1]
    base = sum(p[:, :cols].astype(F32) for p in parts)
    shrink = shrink_sum([p[:, cols:].astype(F32) for p in parts], rank).astype(BF16).astype(F32)
    slots = slot_ref[...]
    mine = mine_ref[0]
    per = up_a.shape[0] // rank
    xa = expanded(slots - mine * per, shrink, rank, up_a.shape[0])
    xb = expanded(slots - (1 - mine) * per, shrink, rank, up_b.shape[0])
    lora = jnp.dot(xa, up_a[...], preferred_element_type=F32) + jnp.dot(
        xb, up_b[...], preferred_element_type=F32
    )
    o_ref[...] = (base + lora).astype(BF16)


def last(mine, slots, up_a, up_b, parts, rank):
    rows, cols = slots.shape[0], up_a.shape[1]
    return call(
        functools.partial(last_body, rank, len(parts)),
        (1,),
        [whole(slots.shape), whole(up_a.shape), whole(up_b.shape)] + [whole(p.shape) for p in parts],
        jax.ShapeDtypeStruct((rows, cols), BF16),
        whole((rows, cols)),
        cost=pl.CostEstimate(flops=4 * rows * up_a.size // rows, bytes_accessed=4 * up_a.size, transcendentals=0),
    )(mine, slots, up_a, up_b, *parts)


def on_device(
    tensor,
    queries,
    cached_key_rows,
    cached_value_rows,
    cache_live_length,
    adapter_index,
    adapter_slot_index,
    output_weight,
    adapter_down_weight,
    adapter_up_weight,
):
    rows, heads, width = queries.shape
    kv_heads, positions = cached_key_rows.shape[1:3]
    group = heads * tensor // kv_heads
    slots_here, _, rank = adapter_down_weight.shape
    cols = adapter_up_weight.shape[2]
    me = lax.axis_index("tensor")
    mine = lax.axis_index("dp")

    def hop(x, k):
        return lax.ppermute(x, "tensor", [(i, i ^ k) for i in range(tensor)])

    def across(x):
        return lax.ppermute(x, "dp", [(0, 1), (1, 0)])

    far = sorted(range(2, tensor, 2), key=lambda k: -min(k, 4))
    outer = far + [0]

    q = queries.reshape(rows * heads, width)
    held = {0: q}
    held[1] = hop(q, 1)
    for k in far:
        held[k] = hop(q, k)
    for k in far:
        held[k ^ 1] = hop(held[k], 1)

    down_a = jnp.swapaxes(adapter_down_weight, 1, 2).reshape(slots_here * rank, -1)
    up_a = adapter_up_weight.reshape(slots_here * rank, cols)
    down_b, up_b = across(down_a), across(up_a)

    live = jnp.clip(cache_live_length - me * positions, 0, positions)
    live = jnp.broadcast_to(jnp.repeat(live, heads)[:, None], (rows * heads, LANES)).astype(jnp.int32)
    scale = 1.0 / math.sqrt(width)
    keys, values, weight = (
        pltpu.with_memory_space_constraint(x, pltpu.HBM)
        for x in (cached_key_rows, cached_value_rows, output_weight)
    )

    def attended(*ks):
        which = jnp.stack([lax.div((me ^ k) * heads, group) for k in ks]).astype(jnp.int32)
        return attend(which, [held[k] for k in ks], live, keys, values, heads, scale)

    partial = dict(zip([1, 0], attended(1, 0)))
    partial.update(zip(far, attended(*far)))
    for k in far:
        (partial[k ^ 1],) = attended(k ^ 1)
    sent = {k: hop(partial[k ^ 1], 1) for k in [0] + far}
    merged = {k: pair(partial[k], sent[k]) for k in [0] + far}
    parts = [merged[0]] + [hop(merged[k], k) for k in far]

    total_slots = adapter_slot_index.shape[0]
    match = adapter_index[:, None] == jnp.arange(total_slots, dtype=jnp.int32)[None, :]
    slot = jnp.sum(jnp.where(match, adapter_slot_index[None, :], 0), axis=1)
    slots = jnp.broadcast_to(slot[:, None], (rows, LANES)).astype(jnp.int32)

    order = jnp.array([k for k in outer], jnp.int32)
    to_pair = jnp.concatenate([mine[None], me ^ order ^ 1]).astype(jnp.int32)
    to_own = jnp.concatenate([mine[None], me ^ order]).astype(jnp.int32)
    first, att, shrink = project(to_pair, parts, weight, slots, down_a, down_b, heads, rank, cols)
    arrived = [hop(x, 1) for x in first]
    own = project_more(to_own, att, shrink, weight, cols)
    summed = [add(a, b, rank) for a, b in zip(own, arrived)]
    final = [hop(x, k) if k else x for x, k in zip(summed, outer)]
    return last(mine[None].astype(jnp.int32), slots, up_a, up_b, final, rank)


def solution(mesh):
    placed = (
        P(("parts", "dp"), "tensor", None),
        P(("parts", "dp"), None, "tensor", None),
        P(("parts", "dp"), None, "tensor", None),
        P(("parts", "dp")),
        P(("parts", "dp")),
        P(),
        P("tensor", None),
        P("dp", "tensor", None),
        P("dp", None, "tensor"),
    )
    return jax.shard_map(
        functools.partial(on_device, mesh.shape["tensor"]),
        mesh=mesh,
        in_specs=placed,
        out_specs=P(("parts", "dp"), "tensor"),
        check_vma=False,
    )
```

```python
import functools
import math

import jax
import jax.numpy as jnp
from jax import lax
from jax.experimental import pallas as pl
from jax.experimental.pallas import tpu as pltpu
from jax.sharding import PartitionSpec as P

F32, BF16 = jnp.float32, jnp.bfloat16
DEAD = -1e30
LANES = 128
TILE = 16
SMALL = 8 * 1024 * 1024
LARGE = 16 * 1024 * 1024


PLAN = [
    ("send", 4, 2, 1),
    ("attend", 0),
    ("forward", 5, 6, 3),
    ("attend", 1, 2, 4),
    ("forward", 7),
    ("attend", 3, 5),
    ("attend", 7),
    ("attend", 6),
]


def call(body, grid, in_specs, out_shape, out_specs, scratch=(), prefetch=1, cost=None):
    return pl.pallas_call(
        body,
        grid_spec=pltpu.PrefetchScalarGridSpec(
            num_scalar_prefetch=prefetch,
            grid=grid,
            in_specs=in_specs,
            out_specs=out_specs,
            scratch_shapes=list(scratch),
        ),
        out_shape=out_shape,
        compiler_params=pltpu.CompilerParams(vmem_limit_bytes=SMALL),
        cost_estimate=cost,
    )


def whole(shape):
    return pl.BlockSpec(shape, lambda i, *_: (0,) * len(shape))


def split2(x):
    high = x.astype(BF16).astype(F32)
    return high, (x - high).astype(BF16).astype(F32)


def iota(shape, dim):
    return lax.broadcasted_iota(jnp.int32, shape, dim)


def attend_part(heads, scale, q, lengths, keys, values, first_tile, o_ref):
    rows, positions = keys.shape[0], keys.shape[1]
    per_tile = TILE // heads
    tiles = rows // per_tile
    row = iota((TILE, LANES), 0) // heads
    lane = iota((TILE, LANES), 1)
    owner = iota((TILE, positions), 0) // heads
    scores, live = [], []
    for g in range(tiles):
        bound = jnp.zeros((TILE, positions), jnp.int32)
        for a in range(per_tile):
            bound = jnp.where(owner == a, lengths[(first_tile + g) * per_tile + a], bound)
        live.append(bound)
        left = q[g * TILE : (g + 1) * TILE, :]
        zero = jnp.zeros_like(left)
        left = jnp.concatenate([jnp.where(row == a, left, zero) for a in range(per_tile)], axis=1)
        right = jnp.concatenate([keys[g * per_tile + a] for a in range(per_tile)], axis=1)
        scores.append(
            lax.dot_general(left, right, (((1,), (1,)), ((), ())), preferred_element_type=F32)
        )
    s = jnp.concatenate(scores, axis=0) * scale
    alive = iota(s.shape, 1) < jnp.concatenate(live, axis=0)
    s = jnp.where(alive, s, DEAD)
    high, mid = split2(jnp.max(s, axis=1, keepdims=True))
    p = jnp.where(alive, jnp.exp(s - (high + mid)), 0.0)
    lhigh, lmid = split2(jnp.sum(p, axis=1, keepdims=True))
    p = p.astype(BF16)
    stat = jnp.zeros((TILE, LANES), F32)
    for g in range(tiles):
        at = slice(g * TILE, (g + 1) * TILE)
        right = jnp.concatenate([values[g * per_tile + a] for a in range(per_tile)], axis=1)
        wide = jnp.dot(p[at], right, preferred_element_type=F32)
        acc = wide[:, :LANES]
        for a in range(1, per_tile):
            acc = jnp.where(row == a, wide[:, a * LANES : (a + 1) * LANES], acc)
        to = first_tile + g
        o_ref[to * TILE : (to + 1) * TILE, :] = acc.astype(BF16)
        for n, val in enumerate((high, mid, lhigh, lmid)):
            stat = jnp.where(lane == 4 * to + n, val[at], stat)
    return stat


def attend_body(n, blocks, heads, scale, sc_ref, len_ref, k_hbm, v_hbm, *refs):
    q_refs = refs[:n]
    o_refs = refs[-6 - n : -6]
    q_buf, k_buf, v_buf, q_sem, k_sem, v_sem = refs[-6:]
    size = k_hbm.shape[0] // blocks
    many = size * heads
    first, copies = [], []
    for j in range(n):
        kv = sc_ref[j]
        first.append(pltpu.make_async_copy(q_refs[j], q_buf.at[j], q_sem.at[j]))
        for b in range(blocks):
            at, i = pl.ds(b * size, size), j * blocks + b
            copies.append(
                (
                    pltpu.make_async_copy(k_hbm.at[at, kv], k_buf.at[i], k_sem.at[i]),
                    pltpu.make_async_copy(v_hbm.at[at, kv], v_buf.at[i], v_sem.at[i]),
                )
            )
    for c in first:
        c.start()
    for ck, cv in copies:
        ck.start()
        cv.start()
    for c in first:
        c.wait()
    for j in range(n):
        stat = jnp.zeros((TILE, LANES), F32)
        for b in range(blocks):
            i = j * blocks + b
            copies[i][0].wait()
            copies[i][1].wait()
            stat = stat + attend_part(
                heads, scale, q_buf[j, b * many : (b + 1) * many, :], len_ref, k_buf.at[i], v_buf.at[i],
                b * many // TILE, o_refs[j],
            )
        o_refs[j][many * blocks :, :] = stat.astype(BF16)


def attend(which, queries, live, keys, values, heads, scale, after):
    n, blocks = len(queries), 2
    rows, _, positions, width = keys.shape
    vmem = pl.BlockSpec(memory_space=pltpu.VMEM)
    smem = pl.BlockSpec(memory_space=pltpu.SMEM)
    hbm = pl.BlockSpec(memory_space=pltpu.HBM)
    anywhere = pl.BlockSpec(memory_space=pl.ANY)
    buf = pltpu.VMEM((n * blocks, rows // blocks, positions, width), BF16)
    sem = pltpu.SemaphoreType.DMA((n * blocks,))
    return pl.pallas_call(
        functools.partial(attend_body, n, blocks, heads, scale),
        in_specs=[smem, smem, hbm, hbm] + [anywhere] * (n + len(after)),
        out_specs=[vmem] * n,
        out_shape=[jax.ShapeDtypeStruct((rows * heads + TILE, width), BF16)] * n,
        scratch_shapes=[
            pltpu.VMEM((n, rows * heads, width), BF16), buf, buf, pltpu.SemaphoreType.DMA((n,)), sem, sem
        ],
        compiler_params=pltpu.CompilerParams(vmem_limit_bytes=LARGE),
        cost_estimate=pl.CostEstimate(
            flops=32 * n * rows * heads * positions * width,
            bytes_accessed=4 * n * rows * positions * width,
            transcendentals=n * rows * heads * positions,
        ),
    )(which, live, keys, values, *queries, *after)


def load_body(blocks, source, *refs):
    target, sem = refs[-2:]
    size = source.shape[0] // blocks
    copies = [
        pltpu.make_async_copy(source.at[pl.ds(b * size, size)], target.at[pl.ds(b * size, size)], sem.at[b])
        for b in range(blocks)
    ]
    for c in copies:
        c.start()
    for c in copies:
        c.wait()


def load(array, after):
    blocks = 4
    return pl.pallas_call(
        functools.partial(load_body, blocks),
        in_specs=[pl.BlockSpec(memory_space=pltpu.HBM)] + [pl.BlockSpec(memory_space=pl.ANY)] * len(after),
        out_specs=pl.BlockSpec(memory_space=pltpu.VMEM),
        out_shape=pltpu.VMEM(array.shape, array.dtype),
        scratch_shapes=[pltpu.SemaphoreType.DMA((blocks,))],
        compiler_params=pltpu.CompilerParams(vmem_limit_bytes=SMALL),
        cost_estimate=pl.CostEstimate(flops=0, bytes_accessed=2 * array.size, transcendentals=0),
    )(array, *after)


def combine(stats):
    tops = [s + pltpu.roll(s, LANES - 1, 1) for s in stats]
    sums = [pltpu.roll(t, LANES - 2, 1) for t in tops]
    best = functools.reduce(jnp.maximum, tops)
    weights = [jnp.exp(t - best) for t in tops]
    total = sum(w * l for w, l in zip(weights, sums))
    return best, weights, total


def pair_body(a_ref, b_ref, o_ref):
    n = a_ref.shape[0] - TILE
    sa = a_ref[pl.ds(n, TILE), :].astype(F32)
    sb = b_ref[pl.ds(n, TILE), :].astype(F32)
    lane = iota((TILE, LANES), 1) % 4
    first = lane == 0
    best, (wa, wb), total = combine([sa, sb])
    wa, wb = jnp.where(first, wa, 0.0), jnp.where(first, wb, 0.0)
    high, mid = split2(best)
    lhigh, lmid = split2(total)
    stat = jnp.where(first, high, 0.0)
    stat = jnp.where(lane == 1, pltpu.roll(mid, 1, 1), stat)
    stat = jnp.where(lane == 2, pltpu.roll(lhigh, 2, 1), stat)
    stat = jnp.where(lane == 3, pltpu.roll(lmid, 3, 1), stat)
    o_ref[pl.ds(n, TILE), :] = stat.astype(BF16)
    for g in range(n // TILE):
        at = pl.ds(g * TILE, TILE)
        o_ref[at, :] = (
            wa[:, 4 * g : 4 * g + 1] * a_ref[at, :].astype(F32)
            + wb[:, 4 * g : 4 * g + 1] * b_ref[at, :].astype(F32)
        ).astype(BF16)


def pair(a, b):
    return pl.pallas_call(
        pair_body,
        out_shape=jax.ShapeDtypeStruct(a.shape, BF16),
        compiler_params=pltpu.CompilerParams(vmem_limit_bytes=SMALL),
        cost_estimate=pl.CostEstimate(flops=3 * a.size, bytes_accessed=6 * a.size, transcendentals=0),
    )(a, b)


def finish_attention(parts, att32, att_ref, heads):
    n = parts[0].shape[0] - TILE
    stats = [p[pl.ds(n, TILE), :].astype(F32) for p in parts]
    _, weights, total = combine(stats)
    inverse = 1.0 / total
    weights = [w * inverse for w in weights]
    for g in range(n // TILE):
        at = pl.ds(g * TILE, TILE)
        att32[at, :] = sum(
            w[:, 4 * g : 4 * g + 1] * p[at, :].astype(F32) for w, p in zip(weights, parts)
        )
    for h in range(heads):
        att_ref[:, h * LANES : (h + 1) * LANES] = att32[pl.ds(h, n // heads, stride=heads), :].astype(BF16)


def chosen(rel, wide, rank):
    total = None
    lane = iota((wide.shape[0], LANES), 1)
    for b in range(wide.shape[1] // LANES):
        part = jnp.where(rel == (lane + b * LANES) // rank, wide[:, b * LANES : (b + 1) * LANES], 0.0)
        total = part if total is None else total + part
    return total


def project_body(n_parts, n_out, heads, rank, sc_ref, *refs):
    parts = refs[:n_parts]
    w_ref, slot_ref, down_a, down_b = refs[n_parts : n_parts + 4]
    outs = refs[n_parts + 4 : n_parts + 4 + n_out]
    att_ref, att32 = refs[n_parts + 4 + n_out :]
    finish_attention(parts, att32, att_ref, heads)
    att = att_ref[...]
    over = (((1,), (1,)), ((), ()))
    own = lax.dot_general(att, down_a[...], over, preferred_element_type=F32)
    other = lax.dot_general(att, down_b[...], over, preferred_element_type=F32)
    slots = slot_ref[...]
    per = down_a.shape[0] // rank
    mine = sc_ref[0]
    s = chosen(slots - mine * per, own, rank) + chosen(slots - (1 - mine) * per, other, rank)
    s = s + pltpu.roll(s, rank, 1)
    high, mid = split2(s)
    shrink = jnp.where(iota(s.shape, 1) < rank, high, mid)
    for k, out in enumerate(outs):
        cols = out.shape[1] - LANES
        at = pl.ds(pl.multiple_of(sc_ref[1 + k] * cols, cols), cols)
        out[:, :cols] = jnp.dot(att, w_ref[:, at], preferred_element_type=F32).astype(out.dtype)
        out[:, cols:] = shrink.astype(out.dtype)


def project(scalars, parts, weight, slots, down_a, down_b, heads, rank, cols):
    n_out = scalars.shape[0] - 1
    rows = slots.shape[0]
    width = weight.shape[0]
    vmem = pl.BlockSpec(memory_space=pltpu.VMEM)
    return pl.pallas_call(
        functools.partial(project_body, len(parts), n_out, heads, rank),
        in_specs=[pl.BlockSpec(memory_space=pltpu.SMEM)] + [vmem] * (len(parts) + 4),
        out_specs=[vmem] * n_out,
        out_shape=[
            jax.ShapeDtypeStruct((rows, cols + LANES), BF16 if k < n_out // 2 else F32)
            for k in range(n_out)
        ],
        scratch_shapes=[pltpu.VMEM((rows, width), BF16), pltpu.VMEM((rows * heads, LANES), F32)],
        compiler_params=pltpu.CompilerParams(vmem_limit_bytes=SMALL),
        cost_estimate=pl.CostEstimate(
            flops=2 * rows * width * cols * n_out, bytes_accessed=2 * width * cols * n_out, transcendentals=0
        ),
    )(scalars, *parts, weight, slots, down_a, down_b)


def shrink_sum(parts, rank):
    both = sum(parts)
    return both + pltpu.roll(both, rank, 1)


def add_body(rank, a_ref, b_ref, o_ref):
    cols = a_ref.shape[1] - LANES
    o_ref[:, :cols] = (a_ref[:, :cols] + b_ref[:, :cols].astype(F32)).astype(BF16)
    s = shrink_sum([a_ref[:, cols:], b_ref[:, cols:].astype(F32)], rank)
    high, mid = split2(s)
    o_ref[:, cols:] = jnp.where(iota(s.shape, 1) < rank, high, mid).astype(BF16)


def add(a, b, rank):
    return pl.pallas_call(
        functools.partial(add_body, rank),
        out_shape=jax.ShapeDtypeStruct(a.shape, BF16),
        compiler_params=pltpu.CompilerParams(vmem_limit_bytes=SMALL),
        cost_estimate=pl.CostEstimate(flops=a.size, bytes_accessed=8 * a.size, transcendentals=0),
    )(a, b)


def expanded(rel, shrink, rank, width):
    lane = iota((rel.shape[0], LANES), 1)
    zero = jnp.zeros(rel.shape, F32)
    return jnp.concatenate(
        [
            jnp.where(rel == (lane + b * LANES) // rank, shrink, zero).astype(BF16)
            for b in range(width // LANES)
        ],
        axis=1,
    )


def last_body(rank, n_parts, mine_ref, slot_ref, up_a, up_b, *refs):
    parts, o_ref = refs[:n_parts], refs[n_parts]
    cols = o_ref.shape[1]
    base = sum(p[:, :cols].astype(F32) for p in parts)
    shrink = shrink_sum([p[:, cols:].astype(F32) for p in parts], rank).astype(BF16).astype(F32)
    slots = slot_ref[...]
    mine = mine_ref[0]
    per = up_a.shape[0] // rank
    xa = expanded(slots - mine * per, shrink, rank, up_a.shape[0])
    xb = expanded(slots - (1 - mine) * per, shrink, rank, up_b.shape[0])
    lora = jnp.dot(xa, up_a[...], preferred_element_type=F32) + jnp.dot(
        xb, up_b[...], preferred_element_type=F32
    )
    o_ref[...] = (base + lora).astype(BF16)


def last(mine, slots, up_a, up_b, parts, rank):
    rows, cols = slots.shape[0], up_a.shape[1]
    return call(
        functools.partial(last_body, rank, len(parts)),
        (1,),
        [whole(slots.shape), whole(up_a.shape), whole(up_b.shape)] + [whole(p.shape) for p in parts],
        jax.ShapeDtypeStruct((rows, cols), BF16),
        whole((rows, cols)),
        cost=pl.CostEstimate(flops=4 * rows * up_a.size // rows, bytes_accessed=4 * up_a.size, transcendentals=0),
    )(mine, slots, up_a, up_b, *parts)


def on_device(
    tensor,
    queries,
    cached_key_rows,
    cached_value_rows,
    cache_live_length,
    adapter_index,
    adapter_slot_index,
    output_weight,
    adapter_down_weight,
    adapter_up_weight,
):
    rows, heads, width = queries.shape
    kv_heads, positions = cached_key_rows.shape[1:3]
    group = heads * tensor // kv_heads
    slots_here, _, rank = adapter_down_weight.shape
    cols = adapter_up_weight.shape[2]
    me = lax.axis_index("tensor")
    mine = lax.axis_index("dp")

    def hop(x, k):
        return lax.ppermute(x, "tensor", [(i, i ^ k) for i in range(tensor)])

    def across(x):
        return lax.ppermute(x, "dp", [(0, 1), (1, 0)])

    far = sorted(range(2, tensor, 2), key=lambda k: -min(k, 4))
    outer = far + [0]

    down_a = jnp.swapaxes(adapter_down_weight, 1, 2).reshape(slots_here * rank, -1)
    up_a = adapter_up_weight.reshape(slots_here * rank, cols)
    down_b, up_b = across(down_a), across(up_a)

    live = jnp.clip(cache_live_length - me * positions, 0, positions).astype(jnp.int32)
    scale = 1.0 / math.sqrt(width)
    keys, values, weight = (
        pltpu.with_memory_space_constraint(x, pltpu.HBM)
        for x in (cached_key_rows, cached_value_rows, output_weight)
    )

    held, partial, token = {0: queries.reshape(rows * heads, width)}, {}, ()
    for kind, *ks in PLAN + [(kind, k) for k in range(8, tensor) for kind in ("forward", "attend")]:
        if kind == "attend":
            which = jnp.stack([lax.div((me ^ k) * heads, group) for k in ks]).astype(jnp.int32)
            outs = attend(which, [held[k] for k in ks], live, keys, values, heads, scale, token)
            partial.update(zip(ks, outs))
            token = [outs[0]]
            continue
        for k in ks:
            bit = 2 if k & 3 == 3 and k > 3 else k & -k
            source = held[k ^ bit]
            if kind == "forward" and token:
                source, token[0] = lax.optimization_barrier((source, token[0]))
            held[k] = hop(source, bit)
    sent = {k: hop(partial[k ^ 1], 1) for k in [0] + far}
    merged = {k: pair(partial[k], sent[k]) for k in [0] + far}
    parts = [merged[0]] + [hop(merged[k], k) for k in far]

    total_slots = adapter_slot_index.shape[0]
    match = adapter_index[:, None] == jnp.arange(total_slots, dtype=jnp.int32)[None, :]
    slot = jnp.sum(jnp.where(match, adapter_slot_index[None, :], 0), axis=1)
    slots = jnp.broadcast_to(slot[:, None], (rows, LANES)).astype(jnp.int32)

    order = jnp.array([k for k in outer], jnp.int32)
    scalars = jnp.concatenate([mine[None], me ^ order ^ 1, me ^ order]).astype(jnp.int32)
    weight = load(weight, [merged[k] for k in far])
    outs = project(scalars, parts, weight, slots, down_a, down_b, heads, rank, cols)
    first, own = outs[: len(outer)], outs[len(outer) :]
    arrived = [hop(x, 1) for x in first]
    summed = [add(a, b, rank) for a, b in zip(own, arrived)]
    final = [hop(x, k) if k else x for x, k in zip(summed, outer)]
    return last(mine[None].astype(jnp.int32), slots, up_a, up_b, final, rank)


def solution(mesh):
    placed = (
        P(("parts", "dp"), "tensor", None),
        P(("parts", "dp"), None, "tensor", None),
        P(("parts", "dp"), None, "tensor", None),
        P(("parts", "dp")),
        P(("parts", "dp")),
        P(),
        P("tensor", None),
        P("dp", "tensor", None),
        P("dp", None, "tensor"),
    )
    return jax.shard_map(
        functools.partial(on_device, mesh.shape["tensor"]),
        mesh=mesh,
        in_specs=placed,
        out_specs=P(("parts", "dp"), "tensor"),
        check_vma=False,
    )
```

```python
import functools
import math

import jax
import jax.numpy as jnp
from jax import lax
from jax.experimental import pallas as pl
from jax.experimental.pallas import tpu as pltpu
from jax.sharding import PartitionSpec as P

F32, BF16 = jnp.float32, jnp.bfloat16
DEAD = -1e30
LANES = 128
TILE = 16
SMALL = 8 * 1024 * 1024
LARGE = 16 * 1024 * 1024


PLAN = [
    ("send", 4, 2, 1),
    ("attend", 0),
    ("forward", 5, 6, 3),
    ("attend", 1, 2, 4),
    ("forward", 7),
    ("attend", 3, 5),
    ("attend", 7, 6),
]


def split2(x):
    high = x.astype(BF16).astype(F32)
    return high, (x - high).astype(BF16).astype(F32)


def iota(shape, dim):
    return lax.broadcasted_iota(jnp.int32, shape, dim)


def attend_part(heads, scale, q, lengths, keys, values, first_tile, o_ref):
    rows, positions = keys.shape[0], keys.shape[1]
    per_tile = TILE // heads
    tiles = rows // per_tile
    row = iota((TILE, LANES), 0) // heads
    lane = iota((TILE, LANES), 1)
    owner = iota((TILE, positions), 0) // heads
    scores, live = [], []
    for g in range(tiles):
        bound = jnp.zeros((TILE, positions), jnp.int32)
        for a in range(per_tile):
            bound = jnp.where(owner == a, lengths[(first_tile + g) * per_tile + a], bound)
        live.append(bound)
        left = q[g * TILE : (g + 1) * TILE, :]
        zero = jnp.zeros_like(left)
        left = jnp.concatenate([jnp.where(row == a, left, zero) for a in range(per_tile)], axis=1)
        right = jnp.concatenate([keys[g * per_tile + a] for a in range(per_tile)], axis=1)
        scores.append(
            lax.dot_general(left, right, (((1,), (1,)), ((), ())), preferred_element_type=F32)
        )
    s = jnp.concatenate(scores, axis=0) * scale
    alive = iota(s.shape, 1) < jnp.concatenate(live, axis=0)
    s = jnp.where(alive, s, DEAD)
    high, mid = split2(jnp.max(s, axis=1, keepdims=True))
    p = jnp.where(alive, jnp.exp(s - (high + mid)), 0.0)
    lhigh, lmid = split2(jnp.sum(p, axis=1, keepdims=True))
    p = p.astype(BF16)
    stat = jnp.zeros((TILE, LANES), F32)
    for g in range(tiles):
        at = slice(g * TILE, (g + 1) * TILE)
        right = jnp.concatenate([values[g * per_tile + a] for a in range(per_tile)], axis=1)
        wide = jnp.dot(p[at], right, preferred_element_type=F32)
        acc = wide[:, :LANES]
        for a in range(1, per_tile):
            acc = jnp.where(row == a, wide[:, a * LANES : (a + 1) * LANES], acc)
        to = first_tile + g
        o_ref[to * TILE : (to + 1) * TILE, :] = acc.astype(BF16)
        for n, val in enumerate((high, mid, lhigh, lmid)):
            stat = jnp.where(lane == 4 * to + n, val[at], stat)
    return stat


def attend_body(which, group, blocks, heads, scale, len_ref, k_hbm, v_hbm, *refs):
    n = len(which)
    me = lax.axis_index("tensor")
    q_refs = refs[:n]
    o_refs = refs[-4 - n : -4]
    k_buf, v_buf, k_sem, v_sem = refs[-4:]
    size = k_hbm.shape[0] // blocks
    many = size * heads
    copies = []
    for j in range(n):
        kv = lax.div((me ^ which[j]) * heads, group)
        for b in range(blocks):
            at, i = pl.ds(b * size, size), j * blocks + b
            copies.append(
                (
                    pltpu.make_async_copy(k_hbm.at[at, kv], k_buf.at[i], k_sem.at[i]),
                    pltpu.make_async_copy(v_hbm.at[at, kv], v_buf.at[i], v_sem.at[i]),
                )
            )
    for ck, cv in copies:
        ck.start()
        cv.start()
    for j in range(n):
        stat = jnp.zeros((TILE, LANES), F32)
        for b in range(blocks):
            i = j * blocks + b
            copies[i][0].wait()
            copies[i][1].wait()
            stat = stat + attend_part(
                heads, scale, q_refs[j][b * many : (b + 1) * many, :], len_ref, k_buf.at[i], v_buf.at[i],
                b * many // TILE, o_refs[j],
            )
        o_refs[j][many * blocks :, :] = stat.astype(BF16)


def attend(which, group, queries, live, keys, values, heads, scale, after):
    n, blocks = len(queries), 2
    rows, _, positions, width = keys.shape
    vmem = pl.BlockSpec(memory_space=pltpu.VMEM)
    smem = pl.BlockSpec(memory_space=pltpu.SMEM)
    hbm = pl.BlockSpec(memory_space=pltpu.HBM)
    anywhere = pl.BlockSpec(memory_space=pl.ANY)
    buf = pltpu.VMEM((n * blocks, rows // blocks, positions, width), BF16)
    sem = pltpu.SemaphoreType.DMA((n * blocks,))
    return pl.pallas_call(
        functools.partial(attend_body, which, group, blocks, heads, scale),
        in_specs=[smem, hbm, hbm] + [vmem] * n + [anywhere] * len(after),
        out_specs=[vmem] * n,
        out_shape=[jax.ShapeDtypeStruct((rows * heads + TILE, width), BF16)] * n,
        scratch_shapes=[buf, buf, sem, sem],
        compiler_params=pltpu.CompilerParams(vmem_limit_bytes=LARGE),
        cost_estimate=pl.CostEstimate(
            flops=32 * n * rows * heads * positions * width,
            bytes_accessed=4 * n * rows * positions * width,
            transcendentals=n * rows * heads * positions,
        ),
    )(live, keys, values, *queries, *after)


def load_body(blocks, source, *refs):
    target, sem = refs[-2:]
    size = source.shape[0] // blocks
    copies = [
        pltpu.make_async_copy(source.at[pl.ds(b * size, size)], target.at[pl.ds(b * size, size)], sem.at[b])
        for b in range(blocks)
    ]
    for c in copies:
        c.start()
    for c in copies:
        c.wait()


def load(array, after):
    blocks = 4
    return pl.pallas_call(
        functools.partial(load_body, blocks),
        in_specs=[pl.BlockSpec(memory_space=pltpu.HBM)] + [pl.BlockSpec(memory_space=pl.ANY)] * len(after),
        out_specs=pl.BlockSpec(memory_space=pltpu.VMEM),
        out_shape=pltpu.VMEM(array.shape, array.dtype),
        scratch_shapes=[pltpu.SemaphoreType.DMA((blocks,))],
        compiler_params=pltpu.CompilerParams(vmem_limit_bytes=SMALL),
        cost_estimate=pl.CostEstimate(flops=0, bytes_accessed=2 * array.size, transcendentals=0),
    )(array, *after)


def combine(stats):
    tops = [s + pltpu.roll(s, LANES - 1, 1) for s in stats]
    sums = [pltpu.roll(t, LANES - 2, 1) for t in tops]
    best = functools.reduce(jnp.maximum, tops)
    weights = [jnp.exp(t - best) for t in tops]
    total = sum(w * l for w, l in zip(weights, sums))
    return best, weights, total


def pair_body(a_ref, b_ref, o_ref):
    n = a_ref.shape[0] - TILE
    sa = a_ref[pl.ds(n, TILE), :].astype(F32)
    sb = b_ref[pl.ds(n, TILE), :].astype(F32)
    lane = iota((TILE, LANES), 1) % 4
    first = lane == 0
    best, (wa, wb), total = combine([sa, sb])
    wa, wb = jnp.where(first, wa, 0.0), jnp.where(first, wb, 0.0)
    high, mid = split2(best)
    lhigh, lmid = split2(total)
    stat = jnp.where(first, high, 0.0)
    stat = jnp.where(lane == 1, pltpu.roll(mid, 1, 1), stat)
    stat = jnp.where(lane == 2, pltpu.roll(lhigh, 2, 1), stat)
    stat = jnp.where(lane == 3, pltpu.roll(lmid, 3, 1), stat)
    o_ref[pl.ds(n, TILE), :] = stat.astype(BF16)
    for g in range(n // TILE):
        at = pl.ds(g * TILE, TILE)
        o_ref[at, :] = (
            wa[:, 4 * g : 4 * g + 1] * a_ref[at, :].astype(F32)
            + wb[:, 4 * g : 4 * g + 1] * b_ref[at, :].astype(F32)
        ).astype(BF16)


def pair(a, b):
    return pl.pallas_call(
        pair_body,
        out_shape=jax.ShapeDtypeStruct(a.shape, BF16),
        compiler_params=pltpu.CompilerParams(vmem_limit_bytes=SMALL),
        cost_estimate=pl.CostEstimate(flops=3 * a.size, bytes_accessed=6 * a.size, transcendentals=0),
    )(a, b)


def finish_attention(parts, att32, att_ref, heads):
    n = parts[0].shape[0] - TILE
    stats = [p[pl.ds(n, TILE), :].astype(F32) for p in parts]
    _, weights, total = combine(stats)
    inverse = 1.0 / total
    weights = [w * inverse for w in weights]
    for g in range(n // TILE):
        at = pl.ds(g * TILE, TILE)
        att32[at, :] = sum(
            w[:, 4 * g : 4 * g + 1] * p[at, :].astype(F32) for w, p in zip(weights, parts)
        )
    for h in range(heads):
        att_ref[:, h * LANES : (h + 1) * LANES] = att32[pl.ds(h, n // heads, stride=heads), :].astype(BF16)


def chosen(rel, wide, rank):
    total = None
    lane = iota((wide.shape[0], LANES), 1)
    for b in range(wide.shape[1] // LANES):
        part = jnp.where(rel == (lane + b * LANES) // rank, wide[:, b * LANES : (b + 1) * LANES], 0.0)
        total = part if total is None else total + part
    return total


def project_body(n_parts, blocks, heads, rank, *refs):
    parts = refs[:n_parts]
    w_ref, slot_ref, down_a, down_b = refs[n_parts : n_parts + 4]
    outs = refs[n_parts + 4 : -2]
    att_ref, att32 = refs[-2:]
    me, mine = lax.axis_index("tensor"), lax.axis_index("dp")
    finish_attention(parts, att32, att_ref, heads)
    att = att_ref[...]
    over = (((1,), (1,)), ((), ()))
    own = lax.dot_general(att, down_a[...], over, preferred_element_type=F32)
    other = lax.dot_general(att, down_b[...], over, preferred_element_type=F32)
    slots = slot_ref[...]
    per = down_a.shape[0] // rank
    s = chosen(slots - mine * per, own, rank) + chosen(slots - (1 - mine) * per, other, rank)
    s = s + pltpu.roll(s, rank, 1)
    high, mid = split2(s)
    shrink = jnp.where(iota(s.shape, 1) < rank, high, mid)
    for k, out in enumerate(outs):
        cols = out.shape[1] - LANES
        at = pl.ds(pl.multiple_of((me ^ blocks[k]) * cols, cols), cols)
        out[:, :cols] = jnp.dot(att, w_ref[:, at], preferred_element_type=F32).astype(out.dtype)
        out[:, cols:] = shrink.astype(out.dtype)


def project(blocks, parts, weight, slots, down_a, down_b, heads, rank, cols):
    n_out = len(blocks)
    rows = slots.shape[0]
    width = weight.shape[0]
    vmem = pl.BlockSpec(memory_space=pltpu.VMEM)
    return pl.pallas_call(
        functools.partial(project_body, len(parts), blocks, heads, rank),
        in_specs=[vmem] * (len(parts) + 4),
        out_specs=[vmem] * n_out,
        out_shape=[
            jax.ShapeDtypeStruct((rows, cols + LANES), BF16 if k < n_out // 2 else F32)
            for k in range(n_out)
        ],
        scratch_shapes=[pltpu.VMEM((rows, width), BF16), pltpu.VMEM((rows * heads, LANES), F32)],
        compiler_params=pltpu.CompilerParams(vmem_limit_bytes=SMALL),
        cost_estimate=pl.CostEstimate(
            flops=2 * rows * width * cols * n_out, bytes_accessed=2 * width * cols * n_out, transcendentals=0
        ),
    )(*parts, weight, slots, down_a, down_b)


def shrink_sum(parts, rank):
    both = sum(parts)
    return both + pltpu.roll(both, rank, 1)


def add_body(rank, a_ref, b_ref, o_ref):
    cols = a_ref.shape[1] - LANES
    o_ref[:, :cols] = (a_ref[:, :cols] + b_ref[:, :cols].astype(F32)).astype(BF16)
    s = shrink_sum([a_ref[:, cols:], b_ref[:, cols:].astype(F32)], rank)
    high, mid = split2(s)
    o_ref[:, cols:] = jnp.where(iota(s.shape, 1) < rank, high, mid).astype(BF16)


def add(a, b, rank):
    return pl.pallas_call(
        functools.partial(add_body, rank),
        out_shape=jax.ShapeDtypeStruct(a.shape, BF16),
        compiler_params=pltpu.CompilerParams(vmem_limit_bytes=SMALL),
        cost_estimate=pl.CostEstimate(flops=a.size, bytes_accessed=8 * a.size, transcendentals=0),
    )(a, b)


def expanded(rel, shrink, rank, width):
    lane = iota((rel.shape[0], LANES), 1)
    zero = jnp.zeros(rel.shape, F32)
    return jnp.concatenate(
        [
            jnp.where(rel == (lane + b * LANES) // rank, shrink, zero).astype(BF16)
            for b in range(width // LANES)
        ],
        axis=1,
    )


def last_body(rank, n_parts, slot_ref, up_a, up_b, *refs):
    parts, o_ref = refs[:n_parts], refs[n_parts]
    cols = o_ref.shape[1]
    base = sum(p[:, :cols].astype(F32) for p in parts)
    shrink = shrink_sum([p[:, cols:].astype(F32) for p in parts], rank).astype(BF16).astype(F32)
    slots = slot_ref[...]
    mine = lax.axis_index("dp")
    per = up_a.shape[0] // rank
    xa = expanded(slots - mine * per, shrink, rank, up_a.shape[0])
    xb = expanded(slots - (1 - mine) * per, shrink, rank, up_b.shape[0])
    lora = jnp.dot(xa, up_a[...], preferred_element_type=F32) + jnp.dot(
        xb, up_b[...], preferred_element_type=F32
    )
    o_ref[...] = (base + lora).astype(BF16)


def last(slots, up_a, up_b, parts, rank):
    rows, cols = slots.shape[0], up_a.shape[1]
    return pl.pallas_call(
        functools.partial(last_body, rank, len(parts)),
        out_shape=jax.ShapeDtypeStruct((rows, cols), BF16),
        compiler_params=pltpu.CompilerParams(vmem_limit_bytes=LARGE),
        cost_estimate=pl.CostEstimate(flops=4 * up_a.size, bytes_accessed=4 * up_a.size, transcendentals=0),
    )(slots, up_a, up_b, *parts)


def on_device(
    tensor,
    queries,
    cached_key_rows,
    cached_value_rows,
    cache_live_length,
    adapter_index,
    adapter_slot_index,
    output_weight,
    adapter_down_weight,
    adapter_up_weight,
):
    rows, heads, width = queries.shape
    kv_heads, positions = cached_key_rows.shape[1:3]
    group = heads * tensor // kv_heads
    slots_here, _, rank = adapter_down_weight.shape
    cols = adapter_up_weight.shape[2]
    me = lax.axis_index("tensor")

    def hop(x, k):
        return lax.ppermute(x, "tensor", [(i, i ^ k) for i in range(tensor)])

    def across(x):
        return lax.ppermute(x, "dp", [(0, 1), (1, 0)])

    far = sorted(range(2, tensor, 2), key=lambda k: -min(k, 4))
    outer = far[::-1] + [0]

    down_a = jnp.swapaxes(adapter_down_weight, 1, 2).reshape(slots_here * rank, -1)
    up_a = adapter_up_weight.reshape(slots_here * rank, cols)
    down_b, up_b = across(down_a), across(up_a)

    live = jnp.clip(cache_live_length - me * positions, 0, positions).astype(jnp.int32)
    scale = 1.0 / math.sqrt(width)
    keys, values, weight = (
        pltpu.with_memory_space_constraint(x, pltpu.HBM)
        for x in (cached_key_rows, cached_value_rows, output_weight)
    )

    q = queries.reshape(rows * heads, width)
    held, partial, token = {0: q}, {}, ()
    for kind, *ks in PLAN + [(kind, k) for k in range(8, tensor) for kind in ("forward", "attend")]:
        if kind == "attend":
            outs = attend(ks, group, [held[k] for k in ks], live, keys, values, heads, scale, token)
            partial.update(zip(ks, outs))
            token = [outs[0]]
            continue
        for k in ks:
            bit = 2 if k & 3 == 3 and k > 3 else k & -k
            source = held[k ^ bit]
            if kind == "forward" and token:
                source, token[0] = lax.optimization_barrier((source, token[0]))
            held[k] = hop(source, bit)
    sent = {k: hop(partial[k ^ 1], 1) for k in [0] + far}
    merged = {k: pair(partial[k], sent[k]) for k in [0] + far}
    parts = [merged[0]] + [hop(merged[k], k) for k in far]

    total_slots = adapter_slot_index.shape[0]
    match = adapter_index[:, None] == jnp.arange(total_slots, dtype=jnp.int32)[None, :]
    slot = jnp.sum(jnp.where(match, adapter_slot_index[None, :], 0), axis=1)
    slots = jnp.broadcast_to(slot[:, None], (rows, LANES)).astype(jnp.int32)

    blocks = [k ^ 1 for k in outer] + list(outer)
    weight = load(weight, [merged[k] for k in far])
    outs = project(blocks, parts, weight, slots, down_a, down_b, heads, rank, cols)
    first, own = outs[: len(outer)], outs[len(outer) :]
    arrived = [hop(x, 1) for x in first]
    summed = [add(a, b, rank) for a, b in zip(own, arrived)]
    final = [hop(x, k) if k else x for x, k in zip(summed, outer)]
    return last(slots, up_a, up_b, final, rank)


def solution(mesh):
    placed = (
        P(("parts", "dp"), "tensor", None),
        P(("parts", "dp"), None, "tensor", None),
        P(("parts", "dp"), None, "tensor", None),
        P(("parts", "dp")),
        P(("parts", "dp")),
        P(),
        P("tensor", None),
        P("dp", "tensor", None),
        P("dp", None, "tensor"),
    )
    return jax.shard_map(
        functools.partial(on_device, mesh.shape["tensor"]),
        mesh=mesh,
        in_specs=placed,
        out_specs=P(("parts", "dp"), "tensor"),
        check_vma=False,
    )
```

```python
import functools
import math

import jax
import jax.numpy as jnp
from jax import lax
from jax.experimental import pallas as pl
from jax.experimental.pallas import tpu as pltpu
from jax.sharding import PartitionSpec as P

F32, BF16 = jnp.float32, jnp.bfloat16
DEAD = -1e30
LANES = 128
TILE = 16
SMALL = 8 * 1024 * 1024
LARGE = 16 * 1024 * 1024


PLAN = [
    ("send", 4, 2, 1),
    ("attend", 0),
    ("forward", 5, 6, 3),
    ("attend", 1, 2, 4),
    ("forward", 7),
    ("attend", 3, 5),
    ("attend", 7, 6),
]


def split2(x):
    high = x.astype(BF16).astype(F32)
    return high, (x - high).astype(BF16).astype(F32)


def iota(shape, dim):
    return lax.broadcasted_iota(jnp.int32, shape, dim)


def attend_part(heads, scale, q, lengths, begin, keys, values, first_tile, o_ref):
    rows, positions = keys.shape[0], keys.shape[1]
    per_tile = TILE // heads
    tiles = rows // per_tile
    row = iota((TILE, LANES), 0) // heads
    lane = iota((TILE, LANES), 1)
    owner = iota((TILE, positions), 0) // heads
    scores, live = [], []
    for g in range(tiles):
        bound = jnp.zeros((TILE, positions), jnp.int32)
        for a in range(per_tile):
            bound = jnp.where(owner == a, lengths[(first_tile + g) * per_tile + a] - begin, bound)
        live.append(bound)
        left = q[g * TILE : (g + 1) * TILE, :]
        zero = jnp.zeros_like(left)
        left = jnp.concatenate([jnp.where(row == a, left, zero) for a in range(per_tile)], axis=1)
        right = jnp.concatenate([keys[g * per_tile + a] for a in range(per_tile)], axis=1)
        scores.append(
            lax.dot_general(left, right, (((1,), (1,)), ((), ())), preferred_element_type=F32)
        )
    s = jnp.concatenate(scores, axis=0) * scale
    alive = iota(s.shape, 1) < jnp.concatenate(live, axis=0)
    s = jnp.where(alive, s, DEAD)
    high, mid = split2(jnp.max(s, axis=1, keepdims=True))
    p = jnp.where(alive, jnp.exp(s - (high + mid)), 0.0)
    lhigh, lmid = split2(jnp.sum(p, axis=1, keepdims=True))
    p = p.astype(BF16)
    stat = jnp.zeros((TILE, LANES), F32)
    for g in range(tiles):
        at = slice(g * TILE, (g + 1) * TILE)
        right = jnp.concatenate([values[g * per_tile + a] for a in range(per_tile)], axis=1)
        wide = jnp.dot(p[at], right, preferred_element_type=F32)
        acc = wide[:, :LANES]
        for a in range(1, per_tile):
            acc = jnp.where(row == a, wide[:, a * LANES : (a + 1) * LANES], acc)
        to = first_tile + g
        o_ref[to * TILE : (to + 1) * TILE, :] = acc.astype(BF16)
        for n, val in enumerate((high, mid, lhigh, lmid)):
            stat = jnp.where(lane == 4 * to + n, val[at], stat)
    return stat


def attend_body(which, group, blocks, heads, scale, len_ref, k_hbm, v_hbm, *refs):
    n = len(which)
    me = lax.axis_index("tensor")
    q_refs = refs[:n]
    o_refs = refs[-4 - n : -4]
    k_buf, v_buf, k_sem, v_sem = refs[-4:]
    size = k_hbm.shape[0] // blocks
    many = size * heads
    begin = me * k_hbm.shape[2]
    copies = []
    for j in range(n):
        kv = lax.div((me ^ which[j]) * heads, group)
        for b in range(blocks):
            at, i = pl.ds(b * size, size), j * blocks + b
            copies.append(
                (
                    pltpu.make_async_copy(k_hbm.at[at, kv], k_buf.at[i], k_sem.at[i]),
                    pltpu.make_async_copy(v_hbm.at[at, kv], v_buf.at[i], v_sem.at[i]),
                )
            )
    for ck, cv in copies:
        ck.start()
        cv.start()
    for j in range(n):
        stat = jnp.zeros((TILE, LANES), F32)
        for b in range(blocks):
            i = j * blocks + b
            copies[i][0].wait()
            copies[i][1].wait()
            stat = stat + attend_part(
                heads, scale, q_refs[j][b * many : (b + 1) * many, :], len_ref, begin, k_buf.at[i], v_buf.at[i],
                b * many // TILE, o_refs[j],
            )
        o_refs[j][many * blocks :, :] = stat.astype(BF16)


def attend(which, group, queries, live, keys, values, heads, scale, after):
    n, blocks = len(queries), 2
    rows, _, positions, width = keys.shape
    vmem = pl.BlockSpec(memory_space=pltpu.VMEM)
    smem = pl.BlockSpec(memory_space=pltpu.SMEM)
    hbm = pl.BlockSpec(memory_space=pltpu.HBM)
    anywhere = pl.BlockSpec(memory_space=pl.ANY)
    buf = pltpu.VMEM((n * blocks, rows // blocks, positions, width), BF16)
    sem = pltpu.SemaphoreType.DMA((n * blocks,))
    return pl.pallas_call(
        functools.partial(attend_body, which, group, blocks, heads, scale),
        in_specs=[smem, hbm, hbm] + [vmem] * n + [anywhere] * len(after),
        out_specs=[vmem] * n,
        out_shape=[jax.ShapeDtypeStruct((rows * heads + TILE, width), BF16)] * n,
        scratch_shapes=[buf, buf, sem, sem],
        compiler_params=pltpu.CompilerParams(vmem_limit_bytes=LARGE),
        cost_estimate=pl.CostEstimate(
            flops=32 * n * rows * heads * positions * width,
            bytes_accessed=4 * n * rows * positions * width,
            transcendentals=n * rows * heads * positions,
        ),
    )(live, keys, values, *queries, *after)


def load_body(blocks, source, *refs):
    target, sem = refs[-2:]
    size = source.shape[0] // blocks
    copies = [
        pltpu.make_async_copy(source.at[pl.ds(b * size, size)], target.at[pl.ds(b * size, size)], sem.at[b])
        for b in range(blocks)
    ]
    for c in copies:
        c.start()
    for c in copies:
        c.wait()


def load(array, after):
    blocks = 4
    return pl.pallas_call(
        functools.partial(load_body, blocks),
        in_specs=[pl.BlockSpec(memory_space=pltpu.HBM)] + [pl.BlockSpec(memory_space=pl.ANY)] * len(after),
        out_specs=pl.BlockSpec(memory_space=pltpu.VMEM),
        out_shape=pltpu.VMEM(array.shape, array.dtype),
        scratch_shapes=[pltpu.SemaphoreType.DMA((blocks,))],
        compiler_params=pltpu.CompilerParams(vmem_limit_bytes=SMALL),
        cost_estimate=pl.CostEstimate(flops=0, bytes_accessed=2 * array.size, transcendentals=0),
    )(array, *after)


def combine(stats):
    tops = [s + pltpu.roll(s, LANES - 1, 1) for s in stats]
    sums = [pltpu.roll(t, LANES - 2, 1) for t in tops]
    best = functools.reduce(jnp.maximum, tops)
    weights = [jnp.exp(t - best) for t in tops]
    total = sum(w * l for w, l in zip(weights, sums))
    return best, weights, total


def pair_body(a_ref, b_ref, o_ref):
    n = a_ref.shape[0] - TILE
    sa = a_ref[pl.ds(n, TILE), :].astype(F32)
    sb = b_ref[pl.ds(n, TILE), :].astype(F32)
    lane = iota((TILE, LANES), 1) % 4
    first = lane == 0
    best, (wa, wb), total = combine([sa, sb])
    wa, wb = jnp.where(first, wa, 0.0), jnp.where(first, wb, 0.0)
    high, mid = split2(best)
    lhigh, lmid = split2(total)
    stat = jnp.where(first, high, 0.0)
    stat = jnp.where(lane == 1, pltpu.roll(mid, 1, 1), stat)
    stat = jnp.where(lane == 2, pltpu.roll(lhigh, 2, 1), stat)
    stat = jnp.where(lane == 3, pltpu.roll(lmid, 3, 1), stat)
    o_ref[pl.ds(n, TILE), :] = stat.astype(BF16)
    for g in range(n // TILE):
        at = pl.ds(g * TILE, TILE)
        o_ref[at, :] = (
            wa[:, 4 * g : 4 * g + 1] * a_ref[at, :].astype(F32)
            + wb[:, 4 * g : 4 * g + 1] * b_ref[at, :].astype(F32)
        ).astype(BF16)


def pair(a, b):
    return pl.pallas_call(
        pair_body,
        out_shape=jax.ShapeDtypeStruct(a.shape, BF16),
        compiler_params=pltpu.CompilerParams(vmem_limit_bytes=SMALL),
        cost_estimate=pl.CostEstimate(flops=3 * a.size, bytes_accessed=6 * a.size, transcendentals=0),
    )(a, b)


def finish_attention(parts, att32, att_ref, heads):
    n = parts[0].shape[0] - TILE
    stats = [p[pl.ds(n, TILE), :].astype(F32) for p in parts]
    _, weights, total = combine(stats)
    inverse = 1.0 / total
    weights = [w * inverse for w in weights]
    for g in range(n // TILE):
        at = pl.ds(g * TILE, TILE)
        att32[at, :] = sum(
            w[:, 4 * g : 4 * g + 1] * p[at, :].astype(F32) for w, p in zip(weights, parts)
        )
    for h in range(heads):
        att_ref[:, h * LANES : (h + 1) * LANES] = att32[pl.ds(h, n // heads, stride=heads), :].astype(BF16)


def chosen(rel, wide, rank):
    total = None
    lane = iota((wide.shape[0], LANES), 1)
    for b in range(wide.shape[1] // LANES):
        part = jnp.where(rel == (lane + b * LANES) // rank, wide[:, b * LANES : (b + 1) * LANES], 0.0)
        total = part if total is None else total + part
    return total


def project_body(n_parts, blocks, heads, rank, *refs):
    parts = refs[:n_parts]
    w_ref, slot_ref, down_a, down_b = refs[n_parts : n_parts + 4]
    outs = refs[n_parts + 4 : n_parts + 4 + len(blocks)]
    att_ref, shrink_ref, _, att32 = refs[n_parts + 4 + len(blocks) :]
    me, mine = lax.axis_index("tensor"), lax.axis_index("dp")
    finish_attention(parts, att32, att_ref, heads)
    att = att_ref[...]
    over = (((1,), (1,)), ((), ()))
    own = lax.dot_general(att, down_a[...], over, preferred_element_type=F32)
    other = lax.dot_general(att, down_b[...], over, preferred_element_type=F32)
    slots = slot_ref[...]
    per = down_a.shape[0] // rank
    s = chosen(slots - mine * per, own, rank) + chosen(slots - (1 - mine) * per, other, rank)
    s = s + pltpu.roll(s, rank, 1)
    high, mid = split2(s)
    shrink = jnp.where(iota(s.shape, 1) < rank, high, mid).astype(BF16)
    shrink_ref[...] = shrink
    for k, out in enumerate(outs):
        cols = outs[-1].shape[1]
        at = pl.ds(pl.multiple_of((me ^ blocks[k]) * cols, cols), cols)
        out[:, :cols] = jnp.dot(att, w_ref[:, at], preferred_element_type=F32).astype(BF16)
        if k == 0:
            out[:, cols:] = shrink


def project(blocks, parts, weight, slots, down_a, down_b, heads, rank, cols):
    rows = slots.shape[0]
    width = weight.shape[0]
    vmem = pl.BlockSpec(memory_space=pltpu.VMEM)
    return pl.pallas_call(
        functools.partial(project_body, len(parts), blocks, heads, rank),
        in_specs=[vmem] * (len(parts) + 4),
        out_specs=[vmem] * (len(blocks) + 3),
        out_shape=[
            jax.ShapeDtypeStruct((rows, cols + LANES if k == 0 else cols), BF16)
            for k in range(len(blocks))
        ]
        + [
            jax.ShapeDtypeStruct((rows, width), BF16),
            jax.ShapeDtypeStruct((rows, LANES), BF16),
            pltpu.VMEM(weight.shape, BF16),
        ],
        input_output_aliases={len(parts): len(blocks) + 2},
        scratch_shapes=[pltpu.VMEM((rows * heads, LANES), F32)],
        compiler_params=pltpu.CompilerParams(vmem_limit_bytes=SMALL),
        cost_estimate=pl.CostEstimate(
            flops=2 * rows * width * cols * len(blocks),
            bytes_accessed=2 * width * cols * len(blocks),
            transcendentals=0,
        ),
    )(*parts, weight, slots, down_a, down_b)


def project_more_body(blocks, kinds, w_ref, att_ref, *outs):
    me = lax.axis_index("tensor")
    for k, out in zip(blocks, outs):
        cols = out.shape[1]
        at = pl.ds(pl.multiple_of((me ^ k) * cols, cols), cols)
        out[...] = jnp.dot(att_ref[...], w_ref[:, at], preferred_element_type=F32).astype(out.dtype)


def project_more(blocks, kinds, att, weight, cols):
    rows, width = att.shape
    vmem = pl.BlockSpec(memory_space=pltpu.VMEM)
    return pl.pallas_call(
        functools.partial(project_more_body, blocks, kinds),
        in_specs=[vmem, vmem],
        out_specs=[vmem] * len(blocks),
        out_shape=[jax.ShapeDtypeStruct((rows, cols), kind) for kind in kinds],
        compiler_params=pltpu.CompilerParams(vmem_limit_bytes=SMALL),
        cost_estimate=pl.CostEstimate(
            flops=2 * rows * width * cols * len(blocks),
            bytes_accessed=2 * width * cols * len(blocks),
            transcendentals=0,
        ),
    )(weight, att)


def shrink_sum(parts, rank):
    both = sum(parts)
    return both + pltpu.roll(both, rank, 1)


def add_body(rank, a_ref, b_ref, mine_ref, first_ref, o_ref):
    cols = a_ref.shape[1]
    o_ref[:, :cols] = (a_ref[...] + b_ref[:, :cols].astype(F32)).astype(BF16)
    s = shrink_sum([mine_ref[...].astype(F32), first_ref[:, cols:].astype(F32)], rank)
    high, mid = split2(s)
    o_ref[:, cols:] = jnp.where(iota(s.shape, 1) < rank, high, mid).astype(BF16)


def add(a, b, mine, first, rank):
    return pl.pallas_call(
        functools.partial(add_body, rank),
        out_shape=jax.ShapeDtypeStruct(first.shape, BF16),
        compiler_params=pltpu.CompilerParams(vmem_limit_bytes=SMALL),
        cost_estimate=pl.CostEstimate(flops=a.size, bytes_accessed=8 * a.size, transcendentals=0),
    )(a, b, mine, first)


def expanded(rel, shrink, rank, width):
    lane = iota((rel.shape[0], LANES), 1)
    zero = jnp.zeros(rel.shape, F32)
    return jnp.concatenate(
        [
            jnp.where(rel == (lane + b * LANES) // rank, shrink, zero).astype(BF16)
            for b in range(width // LANES)
        ],
        axis=1,
    )


def last_body(rank, n_parts, slot_ref, up_a, up_b, *refs):
    parts, o_ref = refs[:n_parts], refs[n_parts]
    cols = o_ref.shape[1]
    base = sum(p[:, :cols].astype(F32) for p in parts)
    shrink = shrink_sum([p[:, cols:].astype(F32) for p in parts], rank).astype(BF16).astype(F32)
    slots = slot_ref[...]
    mine = lax.axis_index("dp")
    per = up_a.shape[0] // rank
    xa = expanded(slots - mine * per, shrink, rank, up_a.shape[0])
    xb = expanded(slots - (1 - mine) * per, shrink, rank, up_b.shape[0])
    lora = jnp.dot(xa, up_a[...], preferred_element_type=F32) + jnp.dot(
        xb, up_b[...], preferred_element_type=F32
    )
    o_ref[...] = (base + lora).astype(BF16)


def last(slots, up_a, up_b, parts, rank):
    rows, cols = slots.shape[0], up_a.shape[1]
    return pl.pallas_call(
        functools.partial(last_body, rank, len(parts)),
        out_shape=jax.ShapeDtypeStruct((rows, cols), BF16),
        compiler_params=pltpu.CompilerParams(vmem_limit_bytes=LARGE),
        cost_estimate=pl.CostEstimate(flops=4 * up_a.size, bytes_accessed=4 * up_a.size, transcendentals=0),
    )(slots, up_a, up_b, *parts)


def on_device(
    tensor,
    queries,
    cached_key_rows,
    cached_value_rows,
    cache_live_length,
    adapter_index,
    adapter_slot_index,
    output_weight,
    adapter_down_weight,
    adapter_up_weight,
):
    rows, heads, width = queries.shape
    kv_heads, positions = cached_key_rows.shape[1:3]
    group = heads * tensor // kv_heads
    slots_here, _, rank = adapter_down_weight.shape
    cols = adapter_up_weight.shape[2]
    me = lax.axis_index("tensor")

    def hop(x, k):
        return lax.ppermute(x, "tensor", [(i, i ^ k) for i in range(tensor)])

    def across(x):
        return lax.ppermute(x, "dp", [(0, 1), (1, 0)])

    far = sorted(range(2, tensor, 2), key=lambda k: -min(k, 4))
    outer = far[::-1] + [0]

    down_a = jnp.swapaxes(adapter_down_weight, 1, 2).reshape(slots_here * rank, -1)
    up_a = adapter_up_weight.reshape(slots_here * rank, cols)
    down_b, up_b = across(down_a), across(up_a)

    live = cache_live_length.astype(jnp.int32)
    scale = 1.0 / math.sqrt(width)
    keys, values, weight = (
        pltpu.with_memory_space_constraint(x, pltpu.HBM)
        for x in (cached_key_rows, cached_value_rows, output_weight)
    )

    q = queries.reshape(rows * heads, width)
    held, partial, token = {0: q}, {}, ()
    for kind, *ks in PLAN + [(kind, k) for k in range(8, tensor) for kind in ("forward", "attend")]:
        if kind == "attend":
            outs = attend(ks, group, [held[k] for k in ks], live, keys, values, heads, scale, token)
            partial.update(zip(ks, outs))
            token = [outs[0]]
            continue
        for k in ks:
            bit = 2 if k & 3 == 3 and k > 3 else k & -k
            source = held[k ^ bit]
            if kind == "forward" and token:
                source, token[0] = lax.optimization_barrier((source, token[0]))
            held[k] = hop(source, bit)
    sent = {k: hop(partial[k ^ 1], 1) for k in [0] + far}
    merged = {k: pair(partial[k], sent[k]) for k in [0] + far}
    parts = [merged[0]] + [hop(merged[k], k) for k in far]

    total_slots = adapter_slot_index.shape[0]
    match = adapter_index[:, None] == jnp.arange(total_slots, dtype=jnp.int32)[None, :]
    slot = jnp.sum(jnp.where(match, adapter_slot_index[None, :], 0), axis=1)
    slots = jnp.broadcast_to(slot[:, None], (rows, LANES)).astype(jnp.int32)

    weight = load(weight, [merged[k] for k in far])
    order = far + [0]
    ahead = 2
    pairs = [k ^ 1 for k in order]
    *first, att, shrink, weight = project(
        pairs[:ahead], parts, weight, slots, down_a, down_b, heads, rank, cols
    )
    rest = pairs[ahead:] + order
    kinds = [BF16] * (len(pairs) - ahead) + [F32] * len(order)
    more = project_more(rest, kinds, att, weight, cols)
    out = dict(zip(pairs + order, first + list(more)))
    arrived = {k: hop(out[k ^ 1], 1) for k in outer}
    summed = [add(out[k], arrived[k], shrink, arrived[order[0]], rank) for k in outer]
    final = [hop(x, k) if k else x for x, k in zip(summed, outer)]
    return last(slots, up_a, up_b, final, rank)


def solution(mesh):
    placed = (
        P(("parts", "dp"), "tensor", None),
        P(("parts", "dp"), None, "tensor", None),
        P(("parts", "dp"), None, "tensor", None),
        P(("parts", "dp")),
        P(("parts", "dp")),
        P(),
        P("tensor", None),
        P("dp", "tensor", None),
        P("dp", None, "tensor"),
    )
    return jax.shard_map(
        functools.partial(on_device, mesh.shape["tensor"]),
        mesh=mesh,
        in_specs=placed,
        out_specs=P(("parts", "dp"), "tensor"),
        check_vma=False,
    )
```

```python
import functools
import math

import jax
import jax.numpy as jnp
from jax import lax
from jax.experimental import pallas as pl
from jax.experimental.pallas import tpu as pltpu
from jax.sharding import PartitionSpec as P

F32, BF16 = jnp.float32, jnp.bfloat16
DEAD = -1e30
LANES = 128
TILE = 16
SMALL = 8 * 1024 * 1024
LARGE = 16 * 1024 * 1024


PLAN = [
    ("send", 4, 2, 1),
    ("attend", 0),
    ("forward", 5, 6, 3),
    ("attend", 1, 2, 4),
    ("forward", 7),
    ("attend", 3, 5),
    ("attend", 7, 6),
]


def split2(x):
    high = x.astype(BF16).astype(F32)
    return high, (x - high).astype(BF16).astype(F32)


def iota(shape, dim):
    return lax.broadcasted_iota(jnp.int32, shape, dim)


def attend_part(heads, scale, q, lengths, begin, keys, values, first_tile, o_ref):
    rows, positions = keys.shape[0], keys.shape[1]
    per_tile = TILE // heads
    tiles = rows // per_tile
    row = iota((TILE, LANES), 0) // heads
    lane = iota((TILE, LANES), 1)
    owner = iota((TILE, positions), 0) // heads
    scores, live = [], []
    for g in range(tiles):
        bound = jnp.zeros((TILE, positions), jnp.int32)
        for a in range(per_tile):
            bound = jnp.where(owner == a, lengths[(first_tile + g) * per_tile + a] - begin, bound)
        live.append(bound)
        left = q[g * TILE : (g + 1) * TILE, :]
        zero = jnp.zeros_like(left)
        left = jnp.concatenate([jnp.where(row == a, left, zero) for a in range(per_tile)], axis=1)
        right = jnp.concatenate([keys[g * per_tile + a] for a in range(per_tile)], axis=1)
        scores.append(
            lax.dot_general(left, right, (((1,), (1,)), ((), ())), preferred_element_type=F32)
        )
    s = jnp.concatenate(scores, axis=0) * scale
    alive = iota(s.shape, 1) < jnp.concatenate(live, axis=0)
    s = jnp.where(alive, s, DEAD)
    high, mid = split2(jnp.max(s, axis=1, keepdims=True))
    p = jnp.where(alive, jnp.exp(s - (high + mid)), 0.0)
    lhigh, lmid = split2(jnp.sum(p, axis=1, keepdims=True))
    p = p.astype(BF16)
    stat = jnp.zeros((TILE, LANES), F32)
    for g in range(tiles):
        at = slice(g * TILE, (g + 1) * TILE)
        right = jnp.concatenate([values[g * per_tile + a] for a in range(per_tile)], axis=1)
        wide = jnp.dot(p[at], right, preferred_element_type=F32)
        acc = wide[:, :LANES]
        for a in range(1, per_tile):
            acc = jnp.where(row == a, wide[:, a * LANES : (a + 1) * LANES], acc)
        to = first_tile + g
        o_ref[to * TILE : (to + 1) * TILE, :] = acc.astype(BF16)
        for n, val in enumerate((high, mid, lhigh, lmid)):
            stat = jnp.where(lane == 4 * to + n, val[at], stat)
    return stat


def attend_body(which, group, blocks, heads, scale, len_ref, k_hbm, v_hbm, *refs):
    n = len(which)
    me = lax.axis_index("tensor")
    q_refs = refs[:n]
    o_refs = refs[-4 - n : -4]
    k_buf, v_buf, k_sem, v_sem = refs[-4:]
    size = k_hbm.shape[0] // blocks
    many = size * heads
    begin = me * k_hbm.shape[2]
    copies = []
    for j in range(n):
        kv = lax.div((me ^ which[j]) * heads, group)
        for b in range(blocks):
            at, i = pl.ds(b * size, size), j * blocks + b
            copies.append(
                (
                    pltpu.make_async_copy(k_hbm.at[at, kv], k_buf.at[i], k_sem.at[i]),
                    pltpu.make_async_copy(v_hbm.at[at, kv], v_buf.at[i], v_sem.at[i]),
                )
            )
    for ck, cv in copies:
        ck.start()
        cv.start()
    for j in range(n):
        stat = jnp.zeros((TILE, LANES), F32)
        for b in range(blocks):
            i = j * blocks + b
            copies[i][0].wait()
            copies[i][1].wait()
            stat = stat + attend_part(
                heads, scale, q_refs[j][b * many : (b + 1) * many, :], len_ref, begin, k_buf.at[i], v_buf.at[i],
                b * many // TILE, o_refs[j],
            )
        o_refs[j][many * blocks :, :] = stat.astype(BF16)


def attend(which, group, queries, live, keys, values, heads, scale, after):
    n, blocks = len(queries), 2
    rows, _, positions, width = keys.shape
    vmem = pl.BlockSpec(memory_space=pltpu.VMEM)
    smem = pl.BlockSpec(memory_space=pltpu.SMEM)
    hbm = pl.BlockSpec(memory_space=pltpu.HBM)
    anywhere = pl.BlockSpec(memory_space=pl.ANY)
    buf = pltpu.VMEM((n * blocks, rows // blocks, positions, width), BF16)
    sem = pltpu.SemaphoreType.DMA((n * blocks,))
    return pl.pallas_call(
        functools.partial(attend_body, which, group, blocks, heads, scale),
        in_specs=[smem, hbm, hbm] + [vmem] * n + [anywhere] * len(after),
        out_specs=[vmem] * n,
        out_shape=[jax.ShapeDtypeStruct((rows * heads + TILE, width), BF16)] * n,
        scratch_shapes=[buf, buf, sem, sem],
        compiler_params=pltpu.CompilerParams(vmem_limit_bytes=LARGE),
        cost_estimate=pl.CostEstimate(
            flops=32 * n * rows * heads * positions * width,
            bytes_accessed=4 * n * rows * positions * width,
            transcendentals=n * rows * heads * positions,
        ),
    )(live, keys, values, *queries, *after)


def load_body(blocks, source, *refs):
    target, sem = refs[-2:]
    size = source.shape[0] // blocks
    copies = [
        pltpu.make_async_copy(source.at[pl.ds(b * size, size)], target.at[pl.ds(b * size, size)], sem.at[b])
        for b in range(blocks)
    ]
    for c in copies:
        c.start()
    for c in copies:
        c.wait()


def load(array, after):
    blocks = 4
    return pl.pallas_call(
        functools.partial(load_body, blocks),
        in_specs=[pl.BlockSpec(memory_space=pltpu.HBM)] + [pl.BlockSpec(memory_space=pl.ANY)] * len(after),
        out_specs=pl.BlockSpec(memory_space=pltpu.VMEM),
        out_shape=pltpu.VMEM(array.shape, array.dtype),
        scratch_shapes=[pltpu.SemaphoreType.DMA((blocks,))],
        compiler_params=pltpu.CompilerParams(vmem_limit_bytes=SMALL),
        cost_estimate=pl.CostEstimate(flops=0, bytes_accessed=2 * array.size, transcendentals=0),
    )(array, *after)


def combine(stats):
    tops = [s + pltpu.roll(s, LANES - 1, 1) for s in stats]
    sums = [pltpu.roll(t, LANES - 2, 1) for t in tops]
    best = functools.reduce(jnp.maximum, tops)
    weights = [jnp.exp(t - best) for t in tops]
    total = sum(w * l for w, l in zip(weights, sums))
    return best, weights, total


def pair_body(a_ref, b_ref, *refs):
    o_ref = refs[-1]
    n = a_ref.shape[0] - TILE
    sa = a_ref[pl.ds(n, TILE), :].astype(F32)
    sb = b_ref[pl.ds(n, TILE), :].astype(F32)
    lane = iota((TILE, LANES), 1) % 4
    first = lane == 0
    best, (wa, wb), total = combine([sa, sb])
    wa, wb = jnp.where(first, wa, 0.0), jnp.where(first, wb, 0.0)
    high, mid = split2(best)
    lhigh, lmid = split2(total)
    stat = jnp.where(first, high, 0.0)
    stat = jnp.where(lane == 1, pltpu.roll(mid, 1, 1), stat)
    stat = jnp.where(lane == 2, pltpu.roll(lhigh, 2, 1), stat)
    stat = jnp.where(lane == 3, pltpu.roll(lmid, 3, 1), stat)
    o_ref[pl.ds(n, TILE), :] = stat.astype(BF16)
    for g in range(n // TILE):
        at = pl.ds(g * TILE, TILE)
        o_ref[at, :] = (
            wa[:, 4 * g : 4 * g + 1] * a_ref[at, :].astype(F32)
            + wb[:, 4 * g : 4 * g + 1] * b_ref[at, :].astype(F32)
        ).astype(BF16)


def pair(a, b, *after):
    vmem = pl.BlockSpec(memory_space=pltpu.VMEM)
    return pl.pallas_call(
        pair_body,
        in_specs=[vmem, vmem] + [pl.BlockSpec(memory_space=pl.ANY)] * len(after),
        out_specs=vmem,
        out_shape=jax.ShapeDtypeStruct(a.shape, BF16),
        compiler_params=pltpu.CompilerParams(vmem_limit_bytes=SMALL),
        cost_estimate=pl.CostEstimate(flops=3 * a.size, bytes_accessed=6 * a.size, transcendentals=0),
    )(a, b, *after)


def finish_attention(parts, att32, att_ref, heads):
    n = parts[0].shape[0] - TILE
    stats = [p[pl.ds(n, TILE), :].astype(F32) for p in parts]
    _, weights, total = combine(stats)
    inverse = 1.0 / total
    weights = [w * inverse for w in weights]
    for g in range(n // TILE):
        at = pl.ds(g * TILE, TILE)
        att32[at, :] = sum(
            w[:, 4 * g : 4 * g + 1] * p[at, :].astype(F32) for w, p in zip(weights, parts)
        )
    for h in range(heads):
        att_ref[:, h * LANES : (h + 1) * LANES] = att32[pl.ds(h, n // heads, stride=heads), :].astype(BF16)


def chosen(rel, wide, rank):
    total = None
    lane = iota((wide.shape[0], LANES), 1)
    for b in range(wide.shape[1] // LANES):
        part = jnp.where(rel == (lane + b * LANES) // rank, wide[:, b * LANES : (b + 1) * LANES], 0.0)
        total = part if total is None else total + part
    return total


def project_body(n_parts, blocks, heads, rank, *refs):
    parts = refs[:n_parts]
    w_ref, slot_ref, down_a, down_b = refs[n_parts : n_parts + 4]
    outs = refs[n_parts + 4 : n_parts + 4 + len(blocks)]
    att_ref, shrink_ref, _, att32 = refs[n_parts + 4 + len(blocks) :]
    me, mine = lax.axis_index("tensor"), lax.axis_index("dp")
    finish_attention(parts, att32, att_ref, heads)
    att = att_ref[...]
    over = (((1,), (1,)), ((), ()))
    own = lax.dot_general(att, down_a[...], over, preferred_element_type=F32)
    other = lax.dot_general(att, down_b[...], over, preferred_element_type=F32)
    slots = slot_ref[...]
    per = down_a.shape[0] // rank
    s = chosen(slots - mine * per, own, rank) + chosen(slots - (1 - mine) * per, other, rank)
    s = s + pltpu.roll(s, rank, 1)
    high, mid = split2(s)
    shrink = jnp.where(iota(s.shape, 1) < rank, high, mid).astype(BF16)
    shrink_ref[...] = shrink
    for k, out in enumerate(outs):
        cols = outs[-1].shape[1]
        at = pl.ds(pl.multiple_of((me ^ blocks[k]) * cols, cols), cols)
        out[:, :cols] = jnp.dot(att, w_ref[:, at], preferred_element_type=F32).astype(BF16)
        if k == 0:
            out[:, cols:] = shrink


def project(blocks, parts, weight, slots, down_a, down_b, heads, rank, cols):
    rows = slots.shape[0]
    width = weight.shape[0]
    vmem = pl.BlockSpec(memory_space=pltpu.VMEM)
    return pl.pallas_call(
        functools.partial(project_body, len(parts), blocks, heads, rank),
        in_specs=[vmem] * (len(parts) + 4),
        out_specs=[vmem] * (len(blocks) + 3),
        out_shape=[
            jax.ShapeDtypeStruct((rows, cols + LANES if k == 0 else cols), BF16)
            for k in range(len(blocks))
        ]
        + [
            jax.ShapeDtypeStruct((rows, width), BF16),
            jax.ShapeDtypeStruct((rows, LANES), BF16),
            pltpu.VMEM(weight.shape, BF16),
        ],
        input_output_aliases={len(parts): len(blocks) + 2},
        scratch_shapes=[pltpu.VMEM((rows * heads, LANES), F32)],
        compiler_params=pltpu.CompilerParams(vmem_limit_bytes=SMALL),
        cost_estimate=pl.CostEstimate(
            flops=2 * rows * width * cols * len(blocks),
            bytes_accessed=2 * width * cols * len(blocks),
            transcendentals=0,
        ),
    )(*parts, weight, slots, down_a, down_b)


def project_more_body(blocks, kinds, w_ref, att_ref, *outs):
    me = lax.axis_index("tensor")
    for k, out in zip(blocks, outs):
        cols = out.shape[1]
        at = pl.ds(pl.multiple_of((me ^ k) * cols, cols), cols)
        out[...] = jnp.dot(att_ref[...], w_ref[:, at], preferred_element_type=F32).astype(out.dtype)


def project_more(blocks, kinds, att, weight, cols):
    rows, width = att.shape
    vmem = pl.BlockSpec(memory_space=pltpu.VMEM)
    return pl.pallas_call(
        functools.partial(project_more_body, blocks, kinds),
        in_specs=[vmem, vmem],
        out_specs=[vmem] * len(blocks),
        out_shape=[jax.ShapeDtypeStruct((rows, cols), kind) for kind in kinds],
        compiler_params=pltpu.CompilerParams(vmem_limit_bytes=SMALL),
        cost_estimate=pl.CostEstimate(
            flops=2 * rows * width * cols * len(blocks),
            bytes_accessed=2 * width * cols * len(blocks),
            transcendentals=0,
        ),
    )(weight, att)


def shrink_sum(parts, rank):
    both = sum(parts)
    return both + pltpu.roll(both, rank, 1)


def add_body(rank, a_ref, b_ref, mine_ref, first_ref, o_ref):
    cols = a_ref.shape[1]
    o_ref[:, :cols] = (a_ref[...] + b_ref[:, :cols].astype(F32)).astype(BF16)
    s = shrink_sum([mine_ref[...].astype(F32), first_ref[:, cols:].astype(F32)], rank)
    high, mid = split2(s)
    o_ref[:, cols:] = jnp.where(iota(s.shape, 1) < rank, high, mid).astype(BF16)


def add(a, b, mine, first, rank):
    return pl.pallas_call(
        functools.partial(add_body, rank),
        out_shape=jax.ShapeDtypeStruct(first.shape, BF16),
        compiler_params=pltpu.CompilerParams(vmem_limit_bytes=SMALL),
        cost_estimate=pl.CostEstimate(flops=a.size, bytes_accessed=8 * a.size, transcendentals=0),
    )(a, b, mine, first)


def expanded(rel, shrink, rank, width):
    lane = iota((rel.shape[0], LANES), 1)
    zero = jnp.zeros(rel.shape, F32)
    return jnp.concatenate(
        [
            jnp.where(rel == (lane + b * LANES) // rank, shrink, zero).astype(BF16)
            for b in range(width // LANES)
        ],
        axis=1,
    )


def last_body(rank, n_parts, slot_ref, up_a, up_b, *refs):
    parts, o_ref = refs[:n_parts], refs[n_parts]
    cols = o_ref.shape[1]
    base = sum(p[:, :cols].astype(F32) for p in parts)
    shrink = shrink_sum([p[:, cols:].astype(F32) for p in parts], rank).astype(BF16).astype(F32)
    slots = slot_ref[...]
    mine = lax.axis_index("dp")
    per = up_a.shape[0] // rank
    xa = expanded(slots - mine * per, shrink, rank, up_a.shape[0])
    xb = expanded(slots - (1 - mine) * per, shrink, rank, up_b.shape[0])
    lora = jnp.dot(xa, up_a[...], preferred_element_type=F32) + jnp.dot(
        xb, up_b[...], preferred_element_type=F32
    )
    o_ref[...] = (base + lora).astype(BF16)


def last(slots, up_a, up_b, parts, rank):
    rows, cols = slots.shape[0], up_a.shape[1]
    return pl.pallas_call(
        functools.partial(last_body, rank, len(parts)),
        out_shape=jax.ShapeDtypeStruct((rows, cols), BF16),
        compiler_params=pltpu.CompilerParams(vmem_limit_bytes=LARGE),
        cost_estimate=pl.CostEstimate(flops=4 * up_a.size, bytes_accessed=4 * up_a.size, transcendentals=0),
    )(slots, up_a, up_b, *parts)


def on_device(
    tensor,
    queries,
    cached_key_rows,
    cached_value_rows,
    cache_live_length,
    adapter_index,
    adapter_slot_index,
    output_weight,
    adapter_down_weight,
    adapter_up_weight,
):
    rows, heads, width = queries.shape
    kv_heads, positions = cached_key_rows.shape[1:3]
    group = heads * tensor // kv_heads
    slots_here, _, rank = adapter_down_weight.shape
    cols = adapter_up_weight.shape[2]
    me = lax.axis_index("tensor")

    def hop(x, k):
        return lax.ppermute(x, "tensor", [(i, i ^ k) for i in range(tensor)])

    def across(x):
        return lax.ppermute(x, "dp", [(0, 1), (1, 0)])

    far = sorted(range(2, tensor, 2), key=lambda k: -min(k, 4))
    outer = far[::-1] + [0]

    down_a = jnp.swapaxes(adapter_down_weight, 1, 2).reshape(slots_here * rank, -1)
    up_a = adapter_up_weight.reshape(slots_here * rank, cols)
    down_b, up_b = across(down_a), across(up_a)

    live = cache_live_length.astype(jnp.int32)
    scale = 1.0 / math.sqrt(width)
    keys, values, weight = (
        pltpu.with_memory_space_constraint(x, pltpu.HBM)
        for x in (cached_key_rows, cached_value_rows, output_weight)
    )

    q = queries.reshape(rows * heads, width)
    held, partial, token = {0: q}, {}, ()
    for kind, *ks in PLAN + [(kind, k) for k in range(8, tensor) for kind in ("forward", "attend")]:
        if kind == "attend":
            outs = attend(ks, group, [held[k] for k in ks], live, keys, values, heads, scale, token)
            partial.update(zip(ks, outs))
            token = [outs[0]]
            continue
        for k in ks:
            bit = 2 if k & 3 == 3 and k > 3 else k & -k
            source = held[k ^ bit]
            if kind == "forward" and token:
                source, token[0] = lax.optimization_barrier((source, token[0]))
            held[k] = hop(source, bit)
    sent = {k: hop(partial[k ^ 1], 1) for k in [0, *far[1:], far[0]]}
    merged = {}
    for k in far + [0]:
        merged[k] = pair(partial[k], sent[k], *([merged[far[0]]] if k == 2 and k != far[0] else []))
    parts = [merged[0]] + [hop(merged[k], k) for k in far]

    total_slots = adapter_slot_index.shape[0]
    match = adapter_index[:, None] == jnp.arange(total_slots, dtype=jnp.int32)[None, :]
    slot = jnp.sum(jnp.where(match, adapter_slot_index[None, :], 0), axis=1)
    slots = jnp.broadcast_to(slot[:, None], (rows, LANES)).astype(jnp.int32)

    weight = load(weight, [merged[k] for k in far])
    order = far + [0]
    ahead = 2
    pairs = [k ^ 1 for k in order]
    *first, att, shrink, weight = project(
        pairs[:ahead], parts, weight, slots, down_a, down_b, heads, rank, cols
    )
    rest = pairs[ahead:] + order
    kinds = [BF16] * (len(pairs) - ahead) + [F32] * len(order)
    more = project_more(rest, kinds, att, weight, cols)
    out = dict(zip(pairs + order, first + list(more)))
    arrived = {k: hop(out[k ^ 1], 1) for k in outer}
    summed = [add(out[k], arrived[k], shrink, arrived[order[0]], rank) for k in outer]
    final = [hop(x, k) if k else x for x, k in zip(summed, outer)]
    return last(slots, up_a, up_b, final, rank)


def solution(mesh):
    placed = (
        P(("parts", "dp"), "tensor", None),
        P(("parts", "dp"), None, "tensor", None),
        P(("parts", "dp"), None, "tensor", None),
        P(("parts", "dp")),
        P(("parts", "dp")),
        P(),
        P("tensor", None),
        P("dp", "tensor", None),
        P("dp", None, "tensor"),
    )
    return jax.shard_map(
        functools.partial(on_device, mesh.shape["tensor"]),
        mesh=mesh,
        in_specs=placed,
        out_specs=P(("parts", "dp"), "tensor"),
        check_vma=False,
    )
```

```python
import functools
import math

import jax
import jax.numpy as jnp
from jax import lax
from jax.experimental import pallas as pl
from jax.experimental.pallas import tpu as pltpu
from jax.sharding import PartitionSpec as P

F32, BF16 = jnp.float32, jnp.bfloat16
DEAD = -1e30
LANES = 128
TILE = 16
SMALL = 8 * 1024 * 1024
LARGE = 16 * 1024 * 1024


PLAN = [
    ("send", 4, 2, 1),
    ("attend", 0),
    ("forward", 5, 6, 3),
    ("attend", 1, 2, 4),
    ("forward", 7),
    ("attend", 3, 5),
    ("attend", 7, 6),
]

AHEAD = {(1, 2, 4): (3, 5)}


def split2(x):
    high = x.astype(BF16).astype(F32)
    return high, (x - high).astype(BF16).astype(F32)


def iota(shape, dim):
    return lax.broadcasted_iota(jnp.int32, shape, dim)


def attend_part(heads, scale, q, lengths, begin, keys, values, first_tile, o_ref):
    rows, positions = keys.shape[0], keys.shape[1]
    per_tile = TILE // heads
    tiles = rows // per_tile
    row = iota((TILE, LANES), 0) // heads
    lane = iota((TILE, LANES), 1)
    owner = iota((TILE, positions), 0) // heads
    scores, live = [], []
    for g in range(tiles):
        bound = jnp.zeros((TILE, positions), jnp.int32)
        for a in range(per_tile):
            bound = jnp.where(owner == a, lengths[(first_tile + g) * per_tile + a] - begin, bound)
        live.append(bound)
        left = q[g * TILE : (g + 1) * TILE, :]
        zero = jnp.zeros_like(left)
        left = jnp.concatenate([jnp.where(row == a, left, zero) for a in range(per_tile)], axis=1)
        right = jnp.concatenate([keys[g * per_tile + a] for a in range(per_tile)], axis=1)
        scores.append(
            lax.dot_general(left, right, (((1,), (1,)), ((), ())), preferred_element_type=F32)
        )
    s = jnp.concatenate(scores, axis=0) * scale
    alive = iota(s.shape, 1) < jnp.concatenate(live, axis=0)
    s = jnp.where(alive, s, DEAD)
    high, mid = split2(jnp.max(s, axis=1, keepdims=True))
    p = jnp.where(alive, jnp.exp(s - (high + mid)), 0.0)
    lhigh, lmid = split2(jnp.sum(p, axis=1, keepdims=True))
    p = p.astype(BF16)
    stat = jnp.zeros((TILE, LANES), F32)
    for g in range(tiles):
        at = slice(g * TILE, (g + 1) * TILE)
        right = jnp.concatenate([values[g * per_tile + a] for a in range(per_tile)], axis=1)
        wide = jnp.dot(p[at], right, preferred_element_type=F32)
        acc = wide[:, :LANES]
        for a in range(1, per_tile):
            acc = jnp.where(row == a, wide[:, a * LANES : (a + 1) * LANES], acc)
        to = first_tile + g
        o_ref[to * TILE : (to + 1) * TILE, :] = acc.astype(BF16)
        for n, val in enumerate((high, mid, lhigh, lmid)):
            stat = jnp.where(lane == 4 * to + n, val[at], stat)
    return stat


def fetch(which, group, heads, hbm_refs, buffers, sems, blocks):
    me = lax.axis_index("tensor")
    size = hbm_refs[0].shape[0] // blocks
    copies = []
    for j, k in enumerate(which):
        kv = lax.div((me ^ k) * heads, group)
        for b in range(blocks):
            i = j * blocks + b
            copies.append(
                [
                    pltpu.make_async_copy(src.at[pl.ds(b * size, size), kv], dst.at[i], sem.at[i])
                    for src, dst, sem in zip(hbm_refs, buffers, sems)
                ]
            )
    for pair_of in copies:
        for c in pair_of:
            c.start()
    return copies


def attend_body(which, following, given, group, blocks, heads, scale, len_ref, k_hbm, v_hbm, *refs):
    n = len(which)
    refs = list(refs)
    take = lambda count: [refs.pop() for _ in range(count)][::-1]
    next_sems = take(2) if following else []
    own = take(4) if not given else []
    next_bufs = take(2) if following else []
    o_refs = take(n)
    q_refs = refs[:n]
    begin = lax.axis_index("tensor") * k_hbm.shape[2]
    many = k_hbm.shape[0] // blocks * heads
    if given:
        k_buf, v_buf = refs[n : n + 2]
    else:
        k_buf, v_buf = own[:2]
        copies = fetch(which, group, heads, (k_hbm, v_hbm), own[:2], own[2:], blocks)
    if following:
        ahead = fetch(following, group, heads, (k_hbm, v_hbm), next_bufs, next_sems, blocks)
    for j in range(n):
        stat = jnp.zeros((TILE, LANES), F32)
        for b in range(blocks):
            i = j * blocks + b
            if not given:
                for c in copies[i]:
                    c.wait()
            stat = stat + attend_part(
                heads, scale, q_refs[j][b * many : (b + 1) * many, :], len_ref, begin,
                k_buf.at[i], v_buf.at[i], b * many // TILE, o_refs[j],
            )
        o_refs[j][many * blocks :, :] = stat.astype(BF16)
    if following:
        for pair_of in ahead:
            for c in pair_of:
                c.wait()


def attend(which, following, given, group, queries, live, keys, values, heads, scale, after):
    n, blocks = len(queries), 2
    rows, _, positions, width = keys.shape
    vmem = pl.BlockSpec(memory_space=pltpu.VMEM)
    smem = pl.BlockSpec(memory_space=pltpu.SMEM)
    hbm = pl.BlockSpec(memory_space=pltpu.HBM)
    anywhere = pl.BlockSpec(memory_space=pl.ANY)

    def buf(count):
        return pltpu.VMEM((count * blocks, rows // blocks, positions, width), BF16)

    def sem(count):
        return pltpu.SemaphoreType.DMA((count * blocks,))

    scratch = [] if given else [buf(n), buf(n), sem(n), sem(n)]
    more = [buf(len(following))] * 2 if following else []
    if following:
        scratch += [sem(len(following))] * 2
    outs = pl.pallas_call(
        functools.partial(attend_body, which, following, bool(given), group, blocks, heads, scale),
        in_specs=[smem, hbm, hbm] + [vmem] * (n + len(given)) + [anywhere] * len(after),
        out_specs=[vmem] * (n + len(more)),
        out_shape=[jax.ShapeDtypeStruct((rows * heads + TILE, width), BF16)] * n + more,
        scratch_shapes=scratch,
        compiler_params=pltpu.CompilerParams(vmem_limit_bytes=LARGE),
        cost_estimate=pl.CostEstimate(
            flops=32 * n * rows * heads * positions * width,
            bytes_accessed=4 * n * rows * positions * width,
            transcendentals=n * rows * heads * positions,
        ),
    )(live, keys, values, *queries, *given, *after)
    return outs[:n], list(outs[n:])


def load_body(blocks, source, *refs):
    target, sem = refs[-2:]
    size = source.shape[0] // blocks
    copies = [
        pltpu.make_async_copy(source.at[pl.ds(b * size, size)], target.at[pl.ds(b * size, size)], sem.at[b])
        for b in range(blocks)
    ]
    for c in copies:
        c.start()
    for c in copies:
        c.wait()


def load(array, after):
    blocks = 4
    return pl.pallas_call(
        functools.partial(load_body, blocks),
        in_specs=[pl.BlockSpec(memory_space=pltpu.HBM)] + [pl.BlockSpec(memory_space=pl.ANY)] * len(after),
        out_specs=pl.BlockSpec(memory_space=pltpu.VMEM),
        out_shape=pltpu.VMEM(array.shape, array.dtype),
        scratch_shapes=[pltpu.SemaphoreType.DMA((blocks,))],
        compiler_params=pltpu.CompilerParams(vmem_limit_bytes=SMALL),
        cost_estimate=pl.CostEstimate(flops=0, bytes_accessed=2 * array.size, transcendentals=0),
    )(array, *after)


def combine(stats):
    tops = [s + pltpu.roll(s, LANES - 1, 1) for s in stats]
    sums = [pltpu.roll(t, LANES - 2, 1) for t in tops]
    best = functools.reduce(jnp.maximum, tops)
    weights = [jnp.exp(t - best) for t in tops]
    total = sum(w * l for w, l in zip(weights, sums))
    return best, weights, total


def pair_body(a_ref, b_ref, *refs):
    o_ref = refs[-1]
    n = a_ref.shape[0] - TILE
    sa = a_ref[pl.ds(n, TILE), :].astype(F32)
    sb = b_ref[pl.ds(n, TILE), :].astype(F32)
    lane = iota((TILE, LANES), 1) % 4
    first = lane == 0
    best, (wa, wb), total = combine([sa, sb])
    wa, wb = jnp.where(first, wa, 0.0), jnp.where(first, wb, 0.0)
    high, mid = split2(best)
    lhigh, lmid = split2(total)
    stat = jnp.where(first, high, 0.0)
    stat = jnp.where(lane == 1, pltpu.roll(mid, 1, 1), stat)
    stat = jnp.where(lane == 2, pltpu.roll(lhigh, 2, 1), stat)
    stat = jnp.where(lane == 3, pltpu.roll(lmid, 3, 1), stat)
    o_ref[pl.ds(n, TILE), :] = stat.astype(BF16)
    for g in range(n // TILE):
        at = pl.ds(g * TILE, TILE)
        o_ref[at, :] = (
            wa[:, 4 * g : 4 * g + 1] * a_ref[at, :].astype(F32)
            + wb[:, 4 * g : 4 * g + 1] * b_ref[at, :].astype(F32)
        ).astype(BF16)


def pair(a, b, *after):
    vmem = pl.BlockSpec(memory_space=pltpu.VMEM)
    return pl.pallas_call(
        pair_body,
        in_specs=[vmem, vmem] + [pl.BlockSpec(memory_space=pl.ANY)] * len(after),
        out_specs=vmem,
        out_shape=jax.ShapeDtypeStruct(a.shape, BF16),
        compiler_params=pltpu.CompilerParams(vmem_limit_bytes=SMALL),
        cost_estimate=pl.CostEstimate(flops=3 * a.size, bytes_accessed=6 * a.size, transcendentals=0),
    )(a, b, *after)


def finish_attention(parts, att32, att_ref, heads):
    n = parts[0].shape[0] - TILE
    stats = [p[pl.ds(n, TILE), :].astype(F32) for p in parts]
    _, weights, total = combine(stats)
    inverse = 1.0 / total
    weights = [w * inverse for w in weights]
    for g in range(n // TILE):
        at = pl.ds(g * TILE, TILE)
        att32[at, :] = sum(
            w[:, 4 * g : 4 * g + 1] * p[at, :].astype(F32) for w, p in zip(weights, parts)
        )
    for h in range(heads):
        att_ref[:, h * LANES : (h + 1) * LANES] = att32[pl.ds(h, n // heads, stride=heads), :].astype(BF16)


def chosen(rel, wide, rank):
    total = None
    lane = iota((wide.shape[0], LANES), 1)
    for b in range(wide.shape[1] // LANES):
        part = jnp.where(rel == (lane + b * LANES) // rank, wide[:, b * LANES : (b + 1) * LANES], 0.0)
        total = part if total is None else total + part
    return total


def project_body(n_parts, blocks, heads, rank, *refs):
    parts = refs[:n_parts]
    w_ref, slot_ref, down_a, down_b = refs[n_parts : n_parts + 4]
    outs = refs[n_parts + 4 : n_parts + 4 + len(blocks)]
    att_ref, shrink_ref, _, att32 = refs[n_parts + 4 + len(blocks) :]
    me, mine = lax.axis_index("tensor"), lax.axis_index("dp")
    finish_attention(parts, att32, att_ref, heads)
    att = att_ref[...]
    over = (((1,), (1,)), ((), ()))
    own = lax.dot_general(att, down_a[...], over, preferred_element_type=F32)
    other = lax.dot_general(att, down_b[...], over, preferred_element_type=F32)
    slots = slot_ref[...]
    per = down_a.shape[0] // rank
    s = chosen(slots - mine * per, own, rank) + chosen(slots - (1 - mine) * per, other, rank)
    s = s + pltpu.roll(s, rank, 1)
    high, mid = split2(s)
    shrink = jnp.where(iota(s.shape, 1) < rank, high, mid).astype(BF16)
    shrink_ref[...] = shrink
    for k, out in enumerate(outs):
        cols = outs[-1].shape[1]
        at = pl.ds(pl.multiple_of((me ^ blocks[k]) * cols, cols), cols)
        out[:, :cols] = jnp.dot(att, w_ref[:, at], preferred_element_type=F32).astype(BF16)
        if k == 0:
            out[:, cols:] = shrink


def project(blocks, parts, weight, slots, down_a, down_b, heads, rank, cols):
    rows = slots.shape[0]
    width = weight.shape[0]
    vmem = pl.BlockSpec(memory_space=pltpu.VMEM)
    return pl.pallas_call(
        functools.partial(project_body, len(parts), blocks, heads, rank),
        in_specs=[vmem] * (len(parts) + 4),
        out_specs=[vmem] * (len(blocks) + 3),
        out_shape=[
            jax.ShapeDtypeStruct((rows, cols + LANES if k == 0 else cols), BF16)
            for k in range(len(blocks))
        ]
        + [
            jax.ShapeDtypeStruct((rows, width), BF16),
            jax.ShapeDtypeStruct((rows, LANES), BF16),
            pltpu.VMEM(weight.shape, BF16),
        ],
        input_output_aliases={len(parts): len(blocks) + 2},
        scratch_shapes=[pltpu.VMEM((rows * heads, LANES), F32)],
        compiler_params=pltpu.CompilerParams(vmem_limit_bytes=SMALL),
        cost_estimate=pl.CostEstimate(
            flops=2 * rows * width * cols * len(blocks),
            bytes_accessed=2 * width * cols * len(blocks),
            transcendentals=0,
        ),
    )(*parts, weight, slots, down_a, down_b)


def project_more_body(blocks, kinds, w_ref, att_ref, *outs):
    me = lax.axis_index("tensor")
    for k, out in zip(blocks, outs):
        cols = out.shape[1]
        at = pl.ds(pl.multiple_of((me ^ k) * cols, cols), cols)
        out[...] = jnp.dot(att_ref[...], w_ref[:, at], preferred_element_type=F32).astype(out.dtype)


def project_more(blocks, kinds, att, weight, cols):
    rows, width = att.shape
    vmem = pl.BlockSpec(memory_space=pltpu.VMEM)
    return pl.pallas_call(
        functools.partial(project_more_body, blocks, kinds),
        in_specs=[vmem, vmem],
        out_specs=[vmem] * len(blocks),
        out_shape=[jax.ShapeDtypeStruct((rows, cols), kind) for kind in kinds],
        compiler_params=pltpu.CompilerParams(vmem_limit_bytes=SMALL),
        cost_estimate=pl.CostEstimate(
            flops=2 * rows * width * cols * len(blocks),
            bytes_accessed=2 * width * cols * len(blocks),
            transcendentals=0,
        ),
    )(weight, att)


def shrink_sum(parts, rank):
    both = sum(parts)
    return both + pltpu.roll(both, rank, 1)


def add_body(rank, a_ref, b_ref, mine_ref, first_ref, o_ref):
    cols = a_ref.shape[1]
    o_ref[:, :cols] = (a_ref[...] + b_ref[:, :cols].astype(F32)).astype(BF16)
    s = shrink_sum([mine_ref[...].astype(F32), first_ref[:, cols:].astype(F32)], rank)
    high, mid = split2(s)
    o_ref[:, cols:] = jnp.where(iota(s.shape, 1) < rank, high, mid).astype(BF16)


def add(a, b, mine, first, rank):
    return pl.pallas_call(
        functools.partial(add_body, rank),
        out_shape=jax.ShapeDtypeStruct(first.shape, BF16),
        compiler_params=pltpu.CompilerParams(vmem_limit_bytes=SMALL),
        cost_estimate=pl.CostEstimate(flops=a.size, bytes_accessed=8 * a.size, transcendentals=0),
    )(a, b, mine, first)


def expanded(rel, shrink, rank, width):
    lane = iota((rel.shape[0], LANES), 1)
    zero = jnp.zeros(rel.shape, F32)
    return jnp.concatenate(
        [
            jnp.where(rel == (lane + b * LANES) // rank, shrink, zero).astype(BF16)
            for b in range(width // LANES)
        ],
        axis=1,
    )


def last_body(rank, n_parts, slot_ref, up_a, up_b, *refs):
    parts, o_ref = refs[:n_parts], refs[n_parts]
    cols = o_ref.shape[1]
    base = sum(p[:, :cols].astype(F32) for p in parts)
    shrink = shrink_sum([p[:, cols:].astype(F32) for p in parts], rank).astype(BF16).astype(F32)
    slots = slot_ref[...]
    mine = lax.axis_index("dp")
    per = up_a.shape[0] // rank
    xa = expanded(slots - mine * per, shrink, rank, up_a.shape[0])
    xb = expanded(slots - (1 - mine) * per, shrink, rank, up_b.shape[0])
    lora = jnp.dot(xa, up_a[...], preferred_element_type=F32) + jnp.dot(
        xb, up_b[...], preferred_element_type=F32
    )
    o_ref[...] = (base + lora).astype(BF16)


def last(slots, up_a, up_b, parts, rank):
    rows, cols = slots.shape[0], up_a.shape[1]
    return pl.pallas_call(
        functools.partial(last_body, rank, len(parts)),
        out_shape=jax.ShapeDtypeStruct((rows, cols), BF16),
        compiler_params=pltpu.CompilerParams(vmem_limit_bytes=LARGE),
        cost_estimate=pl.CostEstimate(flops=4 * up_a.size, bytes_accessed=4 * up_a.size, transcendentals=0),
    )(slots, up_a, up_b, *parts)


def on_device(
    tensor,
    queries,
    cached_key_rows,
    cached_value_rows,
    cache_live_length,
    adapter_index,
    adapter_slot_index,
    output_weight,
    adapter_down_weight,
    adapter_up_weight,
):
    rows, heads, width = queries.shape
    kv_heads, positions = cached_key_rows.shape[1:3]
    group = heads * tensor // kv_heads
    slots_here, _, rank = adapter_down_weight.shape
    cols = adapter_up_weight.shape[2]
    me = lax.axis_index("tensor")

    def hop(x, k):
        return lax.ppermute(x, "tensor", [(i, i ^ k) for i in range(tensor)])

    def across(x):
        return lax.ppermute(x, "dp", [(0, 1), (1, 0)])

    far = sorted(range(2, tensor, 2), key=lambda k: -min(k, 4))
    outer = far[::-1] + [0]

    down_a = jnp.swapaxes(adapter_down_weight, 1, 2).reshape(slots_here * rank, -1)
    up_a = adapter_up_weight.reshape(slots_here * rank, cols)
    down_b, up_b = across(down_a), across(up_a)

    live = cache_live_length.astype(jnp.int32)
    scale = 1.0 / math.sqrt(width)
    keys, values, weight = (
        pltpu.with_memory_space_constraint(x, pltpu.HBM)
        for x in (cached_key_rows, cached_value_rows, output_weight)
    )

    q = queries.reshape(rows * heads, width)
    held, partial, token = {0: q}, {}, ()
    given = []
    for kind, *ks in PLAN + [(kind, k) for k in range(8, tensor) for kind in ("forward", "attend")]:
        if kind == "attend":
            outs, given = attend(
                ks, AHEAD.get(tuple(ks), ()), given, group, [held[k] for k in ks],
                live, keys, values, heads, scale, token,
            )
            partial.update(zip(ks, outs))
            token = [outs[0]]
            continue
        for k in ks:
            bit = 2 if k & 3 == 3 and k > 3 else k & -k
            source = held[k ^ bit]
            if kind == "forward" and token:
                source, token[0] = lax.optimization_barrier((source, token[0]))
            held[k] = hop(source, bit)
    sent = {k: hop(partial[k ^ 1], 1) for k in [0, *far[1:], far[0]]}
    merged = {}
    for k in far + [0]:
        merged[k] = pair(partial[k], sent[k], *([merged[far[0]]] if k == 2 and k != far[0] else []))
    parts = [merged[0]] + [hop(merged[k], k) for k in far]

    total_slots = adapter_slot_index.shape[0]
    match = adapter_index[:, None] == jnp.arange(total_slots, dtype=jnp.int32)[None, :]
    slot = jnp.sum(jnp.where(match, adapter_slot_index[None, :], 0), axis=1)
    slots = jnp.broadcast_to(slot[:, None], (rows, LANES)).astype(jnp.int32)

    weight = load(weight, [merged[k] for k in far])
    order = far + [0]
    ahead = 2
    pairs = [k ^ 1 for k in order]
    *first, att, shrink, weight = project(
        pairs[:ahead], parts, weight, slots, down_a, down_b, heads, rank, cols
    )
    rest = pairs[ahead:] + order
    kinds = [BF16] * (len(pairs) - ahead) + [F32] * len(order)
    more = project_more(rest, kinds, att, weight, cols)
    out = dict(zip(pairs + order, first + list(more)))
    arrived = {k: hop(out[k ^ 1], 1) for k in outer}
    summed = [add(out[k], arrived[k], shrink, arrived[order[0]], rank) for k in outer]
    final = [hop(x, k) if k else x for x, k in zip(summed, outer)]
    return last(slots, up_a, up_b, final, rank)


def solution(mesh):
    placed = (
        P(("parts", "dp"), "tensor", None),
        P(("parts", "dp"), None, "tensor", None),
        P(("parts", "dp"), None, "tensor", None),
        P(("parts", "dp")),
        P(("parts", "dp")),
        P(),
        P("tensor", None),
        P("dp", "tensor", None),
        P("dp", None, "tensor"),
    )
    return jax.shard_map(
        functools.partial(on_device, mesh.shape["tensor"]),
        mesh=mesh,
        in_specs=placed,
        out_specs=P(("parts", "dp"), "tensor"),
        check_vma=False,
    )
```

```python
import functools
import math

import jax
import jax.numpy as jnp
from jax import lax
from jax.experimental import pallas as pl
from jax.experimental.pallas import tpu as pltpu
from jax.sharding import PartitionSpec as P

F32, BF16 = jnp.float32, jnp.bfloat16
DEAD = -1e30
LANES = 128
TILE = 16
SMALL = 8 * 1024 * 1024
LARGE = 16 * 1024 * 1024


PLAN = [
    ("send", 4, 2, 1),
    ("attend", 0),
    ("forward", 5, 6, 3),
    ("attend", 1, 2, 4),
    ("forward", 7),
    ("attend", 3, 5),
    ("attend", 7, 6),
]

AHEAD = {(1, 2, 4): (3, 5)}


def split2(x):
    high = x.astype(BF16).astype(F32)
    return high, (x - high).astype(BF16).astype(F32)


def iota(shape, dim):
    return lax.broadcasted_iota(jnp.int32, shape, dim)


def attend_part(heads, scale, q, lengths, begin, keys, values, first_tile, o_ref):
    rows, positions = keys.shape[0], keys.shape[1]
    per_tile = TILE // heads
    tiles = rows // per_tile
    row = iota((TILE, LANES), 0) // heads
    lane = iota((TILE, LANES), 1)
    owner = iota((TILE, positions), 0) // heads
    scores, live = [], []
    for g in range(tiles):
        bound = jnp.zeros((TILE, positions), jnp.int32)
        for a in range(per_tile):
            bound = jnp.where(owner == a, lengths[(first_tile + g) * per_tile + a] - begin, bound)
        live.append(bound)
        left = q[g * TILE : (g + 1) * TILE, :]
        zero = jnp.zeros_like(left)
        left = jnp.concatenate([jnp.where(row == a, left, zero) for a in range(per_tile)], axis=1)
        right = jnp.concatenate([keys[g * per_tile + a] for a in range(per_tile)], axis=1)
        scores.append(
            lax.dot_general(left, right, (((1,), (1,)), ((), ())), preferred_element_type=F32)
        )
    s = jnp.concatenate(scores, axis=0) * scale
    alive = iota(s.shape, 1) < jnp.concatenate(live, axis=0)
    s = jnp.where(alive, s, DEAD)
    high, mid = split2(jnp.max(s, axis=1, keepdims=True))
    p = jnp.where(alive, jnp.exp(s - (high + mid)), 0.0)
    lhigh, lmid = split2(jnp.sum(p, axis=1, keepdims=True))
    p = p.astype(BF16)
    stat = jnp.zeros((TILE, LANES), F32)
    for g in range(tiles):
        at = slice(g * TILE, (g + 1) * TILE)
        right = jnp.concatenate([values[g * per_tile + a] for a in range(per_tile)], axis=1)
        wide = jnp.dot(p[at], right, preferred_element_type=F32)
        acc = wide[:, :LANES]
        for a in range(1, per_tile):
            acc = jnp.where(row == a, wide[:, a * LANES : (a + 1) * LANES], acc)
        to = first_tile + g
        o_ref[to * TILE : (to + 1) * TILE, :] = acc.astype(BF16)
        for n, val in enumerate((high, mid, lhigh, lmid)):
            stat = jnp.where(lane == 4 * to + n, val[at], stat)
    return stat


def fetch(which, group, heads, hbm_refs, buffers, sems, blocks):
    me = lax.axis_index("tensor")
    size = hbm_refs[0].shape[0] // blocks
    copies = []
    for j, k in enumerate(which):
        kv = lax.div((me ^ k) * heads, group)
        for b in range(blocks):
            i = j * blocks + b
            copies.append(
                [
                    pltpu.make_async_copy(src.at[pl.ds(b * size, size), kv], dst.at[i], sem.at[i])
                    for src, dst, sem in zip(hbm_refs, buffers, sems)
                ]
            )
    for pair_of in copies:
        for c in pair_of:
            c.start()
    return copies


def attend_body(which, following, given, group, blocks, heads, scale, len_ref, k_hbm, v_hbm, *refs):
    n = len(which)
    refs = list(refs)
    take = lambda count: [refs.pop() for _ in range(count)][::-1]
    next_sems = take(2) if following else []
    own = take(4) if not given else []
    next_bufs = take(2) if following else []
    o_refs = take(n)
    q_refs = refs[:n]
    begin = lax.axis_index("tensor") * k_hbm.shape[2]
    many = k_hbm.shape[0] // blocks * heads
    if given:
        k_buf, v_buf = refs[n : n + 2]
    else:
        k_buf, v_buf = own[:2]
        copies = fetch(which, group, heads, (k_hbm, v_hbm), own[:2], own[2:], blocks)
    if following:
        ahead = fetch(following, group, heads, (k_hbm, v_hbm), next_bufs, next_sems, blocks)
    for j in range(n):
        stat = jnp.zeros((TILE, LANES), F32)
        for b in range(blocks):
            i = j * blocks + b
            if not given:
                for c in copies[i]:
                    c.wait()
            stat = stat + attend_part(
                heads, scale, q_refs[j][b * many : (b + 1) * many, :], len_ref, begin,
                k_buf.at[i], v_buf.at[i], b * many // TILE, o_refs[j],
            )
        o_refs[j][many * blocks :, :] = stat.astype(BF16)
    if following:
        for pair_of in ahead:
            for c in pair_of:
                c.wait()


def attend(which, following, given, group, queries, live, keys, values, heads, scale, after):
    n, blocks = len(queries), 2
    rows, _, positions, width = keys.shape
    vmem = pl.BlockSpec(memory_space=pltpu.VMEM)
    smem = pl.BlockSpec(memory_space=pltpu.SMEM)
    hbm = pl.BlockSpec(memory_space=pltpu.HBM)
    anywhere = pl.BlockSpec(memory_space=pl.ANY)

    def buf(count):
        return pltpu.VMEM((count * blocks, rows // blocks, positions, width), BF16)

    def sem(count):
        return pltpu.SemaphoreType.DMA((count * blocks,))

    scratch = [] if given else [buf(n), buf(n), sem(n), sem(n)]
    more = [buf(len(following))] * 2 if following else []
    if following:
        scratch += [sem(len(following))] * 2
    outs = pl.pallas_call(
        functools.partial(attend_body, which, following, bool(given), group, blocks, heads, scale),
        in_specs=[smem, hbm, hbm] + [vmem] * (n + len(given)) + [anywhere] * len(after),
        out_specs=[vmem] * (n + len(more)),
        out_shape=[jax.ShapeDtypeStruct((rows * heads + TILE, width), BF16)] * n + more,
        scratch_shapes=scratch,
        compiler_params=pltpu.CompilerParams(vmem_limit_bytes=LARGE),
        cost_estimate=pl.CostEstimate(
            flops=32 * n * rows * heads * positions * width,
            bytes_accessed=4 * n * rows * positions * width,
            transcendentals=n * rows * heads * positions,
        ),
    )(live, keys, values, *queries, *given, *after)
    return outs[:n], list(outs[n:])


def load_body(blocks, source, *refs):
    target, sem = refs[-2:]
    size = source.shape[0] // blocks
    copies = [
        pltpu.make_async_copy(source.at[pl.ds(b * size, size)], target.at[pl.ds(b * size, size)], sem.at[b])
        for b in range(blocks)
    ]
    for c in copies:
        c.start()
    for c in copies:
        c.wait()


def load(array, after):
    blocks = 4
    return pl.pallas_call(
        functools.partial(load_body, blocks),
        in_specs=[pl.BlockSpec(memory_space=pltpu.HBM)] + [pl.BlockSpec(memory_space=pl.ANY)] * len(after),
        out_specs=pl.BlockSpec(memory_space=pltpu.VMEM),
        out_shape=pltpu.VMEM(array.shape, array.dtype),
        scratch_shapes=[pltpu.SemaphoreType.DMA((blocks,))],
        compiler_params=pltpu.CompilerParams(vmem_limit_bytes=SMALL),
        cost_estimate=pl.CostEstimate(flops=0, bytes_accessed=2 * array.size, transcendentals=0),
    )(array, *after)


def combine(stats):
    tops = [s + pltpu.roll(s, LANES - 1, 1) for s in stats]
    sums = [pltpu.roll(t, LANES - 2, 1) for t in tops]
    best = functools.reduce(jnp.maximum, tops)
    weights = [jnp.exp(t - best) for t in tops]
    total = sum(w * l for w, l in zip(weights, sums))
    return best, weights, total


def pair_body(a_ref, b_ref, *refs):
    o_ref = refs[-1]
    n = a_ref.shape[0] - TILE
    sa = a_ref[pl.ds(n, TILE), :].astype(F32)
    sb = b_ref[pl.ds(n, TILE), :].astype(F32)
    lane = iota((TILE, LANES), 1) % 4
    first = lane == 0
    best, (wa, wb), total = combine([sa, sb])
    wa, wb = jnp.where(first, wa, 0.0), jnp.where(first, wb, 0.0)
    high, mid = split2(best)
    lhigh, lmid = split2(total)
    stat = jnp.where(first, high, 0.0)
    stat = jnp.where(lane == 1, pltpu.roll(mid, 1, 1), stat)
    stat = jnp.where(lane == 2, pltpu.roll(lhigh, 2, 1), stat)
    stat = jnp.where(lane == 3, pltpu.roll(lmid, 3, 1), stat)
    o_ref[pl.ds(n, TILE), :] = stat.astype(BF16)
    for g in range(n // TILE):
        at = pl.ds(g * TILE, TILE)
        o_ref[at, :] = (
            wa[:, 4 * g : 4 * g + 1] * a_ref[at, :].astype(F32)
            + wb[:, 4 * g : 4 * g + 1] * b_ref[at, :].astype(F32)
        ).astype(BF16)


def pair(a, b, *after):
    vmem = pl.BlockSpec(memory_space=pltpu.VMEM)
    return pl.pallas_call(
        pair_body,
        in_specs=[vmem, vmem] + [pl.BlockSpec(memory_space=pl.ANY)] * len(after),
        out_specs=vmem,
        out_shape=jax.ShapeDtypeStruct(a.shape, BF16),
        compiler_params=pltpu.CompilerParams(vmem_limit_bytes=SMALL),
        cost_estimate=pl.CostEstimate(flops=3 * a.size, bytes_accessed=6 * a.size, transcendentals=0),
    )(a, b, *after)


def finish_attention(parts, att32, att_ref, heads):
    n = parts[0].shape[0] - TILE
    stats = [p[pl.ds(n, TILE), :].astype(F32) for p in parts]
    _, weights, total = combine(stats)
    inverse = 1.0 / total
    weights = [w * inverse for w in weights]
    for g in range(n // TILE):
        at = pl.ds(g * TILE, TILE)
        att32[at, :] = sum(
            w[:, 4 * g : 4 * g + 1] * p[at, :].astype(F32) for w, p in zip(weights, parts)
        )
    for h in range(heads):
        att_ref[:, h * LANES : (h + 1) * LANES] = att32[pl.ds(h, n // heads, stride=heads), :].astype(BF16)


def chosen(rel, wide, rank):
    total = None
    lane = iota((wide.shape[0], LANES), 1)
    for b in range(wide.shape[1] // LANES):
        part = jnp.where(rel == (lane + b * LANES) // rank, wide[:, b * LANES : (b + 1) * LANES], 0.0)
        total = part if total is None else total + part
    return total


def project_body(n_parts, blocks, heads, rank, *refs):
    parts = refs[:n_parts]
    w_ref, slot_ref, down_a, down_b = refs[n_parts : n_parts + 4]
    outs = refs[n_parts + 4 : n_parts + 4 + len(blocks)]
    att_ref, shrink_ref, _, att32 = refs[n_parts + 4 + len(blocks) :]
    me, mine = lax.axis_index("tensor"), lax.axis_index("dp")
    finish_attention(parts, att32, att_ref, heads)
    att = att_ref[...]
    over = (((1,), (1,)), ((), ()))
    own = lax.dot_general(att, down_a[...], over, preferred_element_type=F32)
    other = lax.dot_general(att, down_b[...], over, preferred_element_type=F32)
    slots = slot_ref[...]
    per = down_a.shape[0] // rank
    s = chosen(slots - mine * per, own, rank) + chosen(slots - (1 - mine) * per, other, rank)
    s = s + pltpu.roll(s, rank, 1)
    high, mid = split2(s)
    shrink = jnp.where(iota(s.shape, 1) < rank, high, mid).astype(BF16)
    shrink_ref[...] = shrink
    for k, out in enumerate(outs):
        cols = outs[-1].shape[1]
        at = pl.ds(pl.multiple_of((me ^ blocks[k]) * cols, cols), cols)
        out[:, :cols] = jnp.dot(att, w_ref[:, at], preferred_element_type=F32).astype(BF16)
        if k == 0:
            out[:, cols:] = shrink


def project(blocks, parts, weight, slots, down_a, down_b, heads, rank, cols):
    rows = slots.shape[0]
    width = weight.shape[0]
    vmem = pl.BlockSpec(memory_space=pltpu.VMEM)
    return pl.pallas_call(
        functools.partial(project_body, len(parts), blocks, heads, rank),
        in_specs=[vmem] * (len(parts) + 4),
        out_specs=[vmem] * (len(blocks) + 3),
        out_shape=[
            jax.ShapeDtypeStruct((rows, cols + LANES if k == 0 else cols), BF16)
            for k in range(len(blocks))
        ]
        + [
            jax.ShapeDtypeStruct((rows, width), BF16),
            jax.ShapeDtypeStruct((rows, LANES), BF16),
            pltpu.VMEM(weight.shape, BF16),
        ],
        input_output_aliases={len(parts): len(blocks) + 2},
        scratch_shapes=[pltpu.VMEM((rows * heads, LANES), F32)],
        compiler_params=pltpu.CompilerParams(vmem_limit_bytes=SMALL),
        cost_estimate=pl.CostEstimate(
            flops=2 * rows * width * cols * len(blocks),
            bytes_accessed=2 * width * cols * len(blocks),
            transcendentals=0,
        ),
    )(*parts, weight, slots, down_a, down_b)


def project_more_body(blocks, kinds, w_ref, att_ref, *outs):
    me = lax.axis_index("tensor")
    for k, out in zip(blocks, outs):
        cols = out.shape[1]
        at = pl.ds(pl.multiple_of((me ^ k) * cols, cols), cols)
        out[...] = jnp.dot(att_ref[...], w_ref[:, at], preferred_element_type=F32).astype(out.dtype)


def project_more(blocks, kinds, att, weight, cols):
    rows, width = att.shape
    vmem = pl.BlockSpec(memory_space=pltpu.VMEM)
    return pl.pallas_call(
        functools.partial(project_more_body, blocks, kinds),
        in_specs=[vmem, vmem],
        out_specs=[vmem] * len(blocks),
        out_shape=[jax.ShapeDtypeStruct((rows, cols), kind) for kind in kinds],
        compiler_params=pltpu.CompilerParams(vmem_limit_bytes=SMALL),
        cost_estimate=pl.CostEstimate(
            flops=2 * rows * width * cols * len(blocks),
            bytes_accessed=2 * width * cols * len(blocks),
            transcendentals=0,
        ),
    )(weight, att)


def shrink_sum(parts, rank):
    both = sum(parts)
    return both + pltpu.roll(both, rank, 1)


def add_body(rank, a_ref, b_ref, mine_ref, first_ref, o_ref):
    cols = a_ref.shape[1]
    o_ref[:, :cols] = (a_ref[...] + b_ref[:, :cols].astype(F32)).astype(BF16)
    s = shrink_sum([mine_ref[...].astype(F32), first_ref[:, cols:].astype(F32)], rank)
    high, mid = split2(s)
    o_ref[:, cols:] = jnp.where(iota(s.shape, 1) < rank, high, mid).astype(BF16)


def add(a, b, mine, first, rank):
    return pl.pallas_call(
        functools.partial(add_body, rank),
        out_shape=jax.ShapeDtypeStruct(first.shape, BF16),
        compiler_params=pltpu.CompilerParams(vmem_limit_bytes=SMALL),
        cost_estimate=pl.CostEstimate(flops=a.size, bytes_accessed=8 * a.size, transcendentals=0),
    )(a, b, mine, first)


def expanded(rel, shrink, rank, width):
    lane = iota((rel.shape[0], LANES), 1)
    zero = jnp.zeros(rel.shape, F32)
    return jnp.concatenate(
        [
            jnp.where(rel == (lane + b * LANES) // rank, shrink, zero).astype(BF16)
            for b in range(width // LANES)
        ],
        axis=1,
    )


def last_body(rank, n_parts, slot_ref, up_a, up_b, *refs):
    parts, o_ref = refs[:n_parts], refs[n_parts]
    cols = o_ref.shape[1]
    base = sum(p[:, :cols].astype(F32) for p in parts)
    shrink = shrink_sum([p[:, cols:].astype(F32) for p in parts], rank).astype(BF16).astype(F32)
    slots = slot_ref[...]
    mine = lax.axis_index("dp")
    per = up_a.shape[0] // rank
    xa = expanded(slots - mine * per, shrink, rank, up_a.shape[0])
    xb = expanded(slots - (1 - mine) * per, shrink, rank, up_b.shape[0])
    lora = jnp.dot(xa, up_a[...], preferred_element_type=F32) + jnp.dot(
        xb, up_b[...], preferred_element_type=F32
    )
    o_ref[...] = (base + lora).astype(BF16)


def last(slots, up_a, up_b, parts, rank):
    rows, cols = slots.shape[0], up_a.shape[1]
    return pl.pallas_call(
        functools.partial(last_body, rank, len(parts)),
        out_shape=jax.ShapeDtypeStruct((rows, cols), BF16),
        compiler_params=pltpu.CompilerParams(vmem_limit_bytes=LARGE),
        cost_estimate=pl.CostEstimate(flops=4 * up_a.size, bytes_accessed=4 * up_a.size, transcendentals=0),
    )(slots, up_a, up_b, *parts)


def on_device(
    tensor,
    queries,
    cached_key_rows,
    cached_value_rows,
    cache_live_length,
    adapter_index,
    adapter_slot_index,
    output_weight,
    adapter_down_weight,
    adapter_up_weight,
):
    rows, heads, width = queries.shape
    kv_heads, positions = cached_key_rows.shape[1:3]
    group = heads * tensor // kv_heads
    slots_here, _, rank = adapter_down_weight.shape
    cols = adapter_up_weight.shape[2]
    me = lax.axis_index("tensor")

    def hop(x, k):
        return lax.ppermute(x, "tensor", [(i, i ^ k) for i in range(tensor)])

    def across(x):
        return lax.ppermute(x, "dp", [(0, 1), (1, 0)])

    far = sorted(range(2, tensor, 2), key=lambda k: -min(k, 4))
    outer = far[::-1] + [0]

    down_a = jnp.swapaxes(adapter_down_weight, 1, 2).reshape(slots_here * rank, -1)
    up_a = adapter_up_weight.reshape(slots_here * rank, cols)
    down_b, up_b = across(down_a), across(up_a)

    live = cache_live_length.astype(jnp.int32)
    scale = 1.0 / math.sqrt(width)
    keys, values, weight = (
        pltpu.with_memory_space_constraint(x, pltpu.HBM)
        for x in (cached_key_rows, cached_value_rows, output_weight)
    )

    q = queries.reshape(rows * heads, width)
    held, partial, token = {0: q}, {}, ()
    given = []
    for kind, *ks in PLAN + [(kind, k) for k in range(8, tensor) for kind in ("forward", "attend")]:
        if kind == "attend":
            outs, given = attend(
                ks, AHEAD.get(tuple(ks), ()), given, group, [held[k] for k in ks],
                live, keys, values, heads, scale, token,
            )
            partial.update(zip(ks, outs))
            token = [outs[0]]
            continue
        for k in ks:
            bit = 2 if k & 3 == 3 and k > 3 else k & -k
            source = held[k ^ bit]
            if kind == "forward" and token:
                source, token[0] = lax.optimization_barrier((source, token[0]))
            held[k] = hop(source, bit)
    sent = {k: hop(partial[k ^ 1], 1) for k in [0, *far[1:], far[0]]}
    merged = {}
    for k in far:
        merged[k] = pair(partial[k], sent[k], *([merged[far[0]]] if k == 2 and k != far[0] else []))
    parts = [partial[0], sent[0]] + [hop(merged[k], k) for k in far]

    total_slots = adapter_slot_index.shape[0]
    match = adapter_index[:, None] == jnp.arange(total_slots, dtype=jnp.int32)[None, :]
    slot = jnp.sum(jnp.where(match, adapter_slot_index[None, :], 0), axis=1)
    slots = jnp.broadcast_to(slot[:, None], (rows, LANES)).astype(jnp.int32)

    weight = load(weight, [merged[k] for k in far])
    order = far + [0]
    ahead = 2
    pairs = [k ^ 1 for k in order]
    *first, att, shrink, weight = project(
        pairs[:ahead], parts, weight, slots, down_a, down_b, heads, rank, cols
    )
    rest = pairs[ahead:] + order
    kinds = [BF16] * (len(pairs) - ahead) + [F32] * len(order)
    more = project_more(rest, kinds, att, weight, cols)
    out = dict(zip(pairs + order, first + list(more)))
    arrived = {k: hop(out[k ^ 1], 1) for k in outer}
    summed = [add(out[k], arrived[k], shrink, arrived[order[0]], rank) for k in outer]
    final = [hop(x, k) if k else x for x, k in zip(summed, outer)]
    return last(slots, up_a, up_b, final, rank)


def solution(mesh):
    placed = (
        P(("parts", "dp"), "tensor", None),
        P(("parts", "dp"), None, "tensor", None),
        P(("parts", "dp"), None, "tensor", None),
        P(("parts", "dp")),
        P(("parts", "dp")),
        P(),
        P("tensor", None),
        P("dp", "tensor", None),
        P("dp", None, "tensor"),
    )
    return jax.shard_map(
        functools.partial(on_device, mesh.shape["tensor"]),
        mesh=mesh,
        in_specs=placed,
        out_specs=P(("parts", "dp"), "tensor"),
        check_vma=False,
    )
```
